128 devices in a mesh: aux: 8 (over y, core), orb: 16 (over x, z).
Axes of the slice: x: 4, y: 4, z: 4, core: 2. Of those that a mesh axis runs over, the one named last changes fastest.
Arguments:
- integrals: float32 [2048, 32, 512], P('aux', 'orb'), may hold values from -0.6 to 0.6
- metric: float32 [2048, 2048], P('aux'), may hold values from -1 to 3, as said below
- occ_energy: float32 [32], replicated, may hold values from -1.2 to -0.2
- vir_energy: float32 [512], replicated, may hold values from 0.1 to 2
- pair_orbitals: int32 [256, 2], replicated, may hold values from 0 to 31, as said below
Outputs:
- gradient: float32 [2048, 32, 512], P('aux', 'orb')
The draws below stay inside these ranges and needn't reach their ends.
Inputs may be any that keep to these rules, and one draw needn't show every extreme that they name: metric is exactly symmetric. `pair_orbitals`: the pairs of one patch use at most one orbital from the block of 2 orbitals of each orb index.
All inputs are finite; a program needn't handle non-finite values.
Results may differ from the reference program's by a relative error of at most 0.0003.
Values sent between devices are 32-bit elements; how exact they have to be, the bound alone decides.
No kernel may reach another device: no remote copies, remote signals or barrier semaphores. Data moves between devices by JAX's collectives and lax.ppermute only.
A program may use at most 128 MiB of HBM per device.

```python
import jax
import jax.numpy as jnp
from jax import lax

NV = 512
NAUX = 2048
OCC_DEV = 2
PAIR_DEV = 16
NOCC = 32
N_ORB = 16


def draw_metric(key, part):
    key_diag = jax.random.fold_in(key, 11)
    key_off = jax.random.fold_in(key, 12)
    diagonal = jax.random.uniform(key_diag, (NAUX,), jnp.float32, 0.5, 2.0)
    raw_values = jax.random.normal(key_off, (NAUX, NAUX), jnp.float32) * 0.012
    off_diag = (raw_values + raw_values.T) * 0.5
    identity = jnp.eye(NAUX, dtype=bool)
    return jnp.where(identity, diagonal[:, None], off_diag).astype(jnp.float32)


def draw_pair_orbitals(key, part):
    key_pick = jax.random.fold_in(key, 21)
    key_near = jax.random.fold_in(key, 22)
    key_far = jax.random.fold_in(key, 23)
    pick_table = jax.random.randint(key_pick, (N_ORB, N_ORB), 0, OCC_DEV)
    owner_dev = jnp.arange(N_ORB, dtype=jnp.int32)[:, None]
    near_dev = jnp.clip(owner_dev + jax.random.randint(key_near, (N_ORB, PAIR_DEV), -2, 3), 0, N_ORB - 1)
    far_dev = jax.random.randint(key_far, (N_ORB, PAIR_DEV), 0, N_ORB)
    first_orb = near_dev * OCC_DEV + jnp.take_along_axis(pick_table, near_dev, axis=1)
    second_orb = far_dev * OCC_DEV + jnp.take_along_axis(pick_table, far_dev, axis=1)
    return jnp.stack([first_orb, second_orb], -1).reshape(N_ORB * PAIR_DEV, 2).astype(jnp.int32)


def level_of(own_key, shape, shards, low, high):
    def one(axis_at, blocks):
        steps = jax.random.uniform(jax.random.fold_in(jax.random.fold_in(own_key, 6), axis_at), (blocks,), jnp.float32, low / len(shards), high / len(shards))
        return jnp.repeat(jnp.exp(steps), shape[axis_at] // blocks).reshape((-1,) + (1,) * (len(shape) - axis_at - 1))

    gain = one(*shards[0])
    for cut in shards[1:]:
        gain = gain * one(*cut)
    return gain


def centred(stream_key, shape, spread, reach, split=(), kind=jnp.bfloat16):
    array = jax.random.normal(stream_key, shape, jnp.float32) * spread
    if len(split) > 0:
        array = level_of(stream_key, shape, split, -0.22, 0.18) * array
    return jnp.clip(array, min=-reach, max=reach).astype(kind)


def setup_inputs(seed: int = 0) -> dict:
    keys = jax.random.split(jax.random.key(seed), 6)
    integrals = centred(keys[0], (NAUX, NOCC, NV), 0.1, 0.6, ((0, 8), (1, 16)), jnp.float32)
    metric = draw_metric(jax.random.fold_in(keys[5], 71), 0)
    occ_energy = jnp.clip(jax.random.uniform(keys[2], (NOCC,), jnp.float32, -1.2, -0.2), -1.2, -0.2)
    vir_energy = jnp.clip(jax.random.uniform(keys[3], (NV,), jnp.float32, 0.1, 2.0), 0.1, 2.0)
    pair_orbitals = draw_pair_orbitals(jax.random.fold_in(keys[5], 71), 0)
    return dict(integrals=integrals, metric=metric, occ_energy=occ_energy, vir_energy=vir_energy, pair_orbitals=pair_orbitals)


def reference(integrals, metric, occ_energy, vir_energy, pair_orbitals):
    aux_total, occ_total, vir_total = integrals.shape
    flat_rows = integrals.reshape(aux_total, occ_total * vir_total)
    fitted = jnp.dot(metric.T, flat_rows, precision=lax.Precision.HIGHEST, preferred_element_type=jnp.float32)
    fitted = fitted.reshape(aux_total, occ_total, vir_total)

    def visit_pair(grads, pair_row):
        first_orb = pair_row[0].astype(jnp.int32)
        second_orb = pair_row[1].astype(jnp.int32)
        left_block = lax.dynamic_index_in_dim(fitted, first_orb, 1, keepdims=False)
        right_block = lax.dynamic_index_in_dim(fitted, second_orb, 1, keepdims=False)
        coupling = jnp.dot(left_block.T, right_block, precision=lax.Precision.HIGHEST, preferred_element_type=jnp.float32)
        denominator = vir_energy[:, None] + vir_energy[None, :] - occ_energy[first_orb] - occ_energy[second_orb]
        amplitudes = -coupling / denominator
        to_first = jnp.dot(right_block, amplitudes.T, precision=lax.Precision.HIGHEST, preferred_element_type=jnp.float32)
        to_second = jnp.dot(left_block, amplitudes, precision=lax.Precision.HIGHEST, preferred_element_type=jnp.float32)
        grads = grads.at[:, first_orb].add(to_first)
        grads = grads.at[:, second_orb].add(to_second)
        return grads, None

    start_grads = jnp.zeros((aux_total, occ_total, vir_total), jnp.float32)
    grads, _ = lax.scan(visit_pair, start_grads, pair_orbitals)
    return grads
```

```python
import functools

import jax
import jax.numpy as jnp
from jax import lax
from jax.experimental import pallas as pl
from jax.experimental.pallas import tpu as pltpu
from jax.sharding import PartitionSpec as P

F32 = jnp.float32
LIMIT = 48 * 1024 * 1024


def split(x):
    high = x.astype(jnp.bfloat16)
    return high, (x - high.astype(F32)).astype(jnp.bfloat16)


def dot3(left, right, dims):
    (lh, ll), (rh, rl) = left, right
    dot = lambda a, b: lax.dot_general(a, b, (dims, ((), ())), preferred_element_type=F32)
    return dot(lh, rh) + (dot(lh, rl) + dot(ll, rh))


def first_kernel(slots, left, right, out):
    out[0] = dot3(split(left[0]), split(right[0]), ((0,), (0,)))


def rest_kernel(slots, left0, left1, right0, right1, mixed, last):
    l0, l1, r0, r1 = (split(x[0]) for x in (left0, left1, right0, right1))
    rows = ((0,), (0,))
    mixed[0, 0] = dot3(l0, r1, rows)
    mixed[1, 0] = dot3(l1, r0, rows)
    last[0] = dot3(l1, r1, rows)


def block_of(side, rows, width):
    return pl.BlockSpec((1, rows, width), lambda p, slots: (slots[side, p], 0, 0))


def first_couplings(slots, half):
    _, rows, width = half.shape
    pairs = slots.shape[1]
    return pl.pallas_call(
        first_kernel,
        grid_spec=pltpu.PrefetchScalarGridSpec(
            num_scalar_prefetch=1,
            grid=(pairs,),
            in_specs=[block_of(0, rows, width), block_of(1, rows, width)],
            out_specs=pl.BlockSpec((1, width, width), lambda p, slots: (p, 0, 0)),
        ),
        out_shape=jax.ShapeDtypeStruct((pairs, width, width), F32),
        compiler_params=pltpu.CompilerParams(vmem_limit_bytes=LIMIT),
    )(slots, half, half)


def rest_couplings(slots, half0, half1):
    _, rows, width = half0.shape
    pairs = slots.shape[1]
    return pl.pallas_call(
        rest_kernel,
        grid_spec=pltpu.PrefetchScalarGridSpec(
            num_scalar_prefetch=1,
            grid=(pairs,),
            in_specs=[
                block_of(0, rows, width),
                block_of(0, rows, width),
                block_of(1, rows, width),
                block_of(1, rows, width),
            ],
            out_specs=[
                pl.BlockSpec((2, 1, width, width), lambda p, slots: (0, p, 0, 0)),
                pl.BlockSpec((1, width, width), lambda p, slots: (p, 0, 0)),
            ],
        ),
        out_shape=[
            jax.ShapeDtypeStruct((2, pairs, width, width), F32),
            jax.ShapeDtypeStruct((pairs, width, width), F32),
        ],
        compiler_params=pltpu.CompilerParams(vmem_limit_bytes=LIMIT),
    )(slots, half0, half1, half0, half1)


def gradient_kernel(
    half, slots, shift, column, row, left0, left1, right0, right1, diagonal, mixed, out
):
    p = pl.program_id(0)
    width = out.shape[2]

    @pl.when(p == 0)
    def _():
        out[...] = jnp.zeros_like(out)

    def amplitude(coupling, first, second):
        down = column[first * width : (first + 1) * width, :]
        along = row[:, second * width : (second + 1) * width]
        return split(-coupling / (down + along - shift[p]))

    lefts = [split(left0[0]), split(left1[0])]
    rights = [split(right0[0]), split(right1[0])]
    other = 1 - half
    same = amplitude(diagonal[0], half, half)
    across = amplitude(mixed[half, 0], half, other)
    down = amplitude(mixed[other, 0], other, half)
    to_first = dot3(rights[half], same, ((1,), (1,))) + dot3(rights[other], across, ((1,), (1,)))
    to_second = dot3(lefts[half], same, ((1,), (0,))) + dot3(lefts[other], down, ((1,), (0,)))
    first, second = slots[0, p], slots[1, p]
    out[first] += to_first
    out[second] += to_second


def gradient_half(half, slots, shift, vir, half0, half1, diagonal, mixed):
    count, rows, width = half0.shape
    pairs = slots.shape[1]
    whole = lambda shape: pl.BlockSpec(shape, lambda p, slots: (0,) * len(shape))
    return pl.pallas_call(
        functools.partial(gradient_kernel, half),
        grid_spec=pltpu.PrefetchScalarGridSpec(
            num_scalar_prefetch=1,
            grid=(pairs,),
            in_specs=[
                pl.BlockSpec(memory_space=pltpu.SMEM),
                whole((vir.shape[0], 1)),
                whole((1, vir.shape[0])),
                block_of(0, rows, width),
                block_of(0, rows, width),
                block_of(1, rows, width),
                block_of(1, rows, width),
                pl.BlockSpec((1, width, width), lambda p, slots: (p, 0, 0)),
                pl.BlockSpec((2, 1, width, width), lambda p, slots: (0, p, 0, 0)),
            ],
            out_specs=whole((count, rows, width)),
        ),
        out_shape=jax.ShapeDtypeStruct((count, rows, width), F32),
        compiler_params=pltpu.CompilerParams(vmem_limit_bytes=LIMIT),
    )(slots, shift, vir[:, None], vir[None, :], half0, half1, half0, half1, diagonal, mixed)


def body(integrals, metric, occ_energy, vir_energy, pair_orbitals):
    rows, occ_count, vir_count = integrals.shape
    width = vir_count // 2
    orb_count = lax.axis_size("orb")
    aux_count = lax.axis_size("aux")
    my_index = lax.axis_index("orb")
    pair_count = pair_orbitals.shape[0] // orb_count
    pair_ends = pair_orbitals.reshape(orb_count, 2 * pair_count)
    local_pick = jnp.where(pair_ends // occ_count == my_index, pair_ends % occ_count, -1)
    wanted = jnp.max(local_pick, axis=1)
    my_pairs = lax.dynamic_slice_in_dim(pair_orbitals, my_index * pair_count, pair_count, 0)
    slots = (my_pairs // occ_count).T
    shift = occ_energy[my_pairs[:, 0]] + occ_energy[my_pairs[:, 1]]

    def gather(h):
        mine = integrals[:, :, h * width : (h + 1) * width].reshape(rows, occ_count * width)
        return lax.all_gather(mine, "aux", axis=0, tiled=True)

    def fit(every):
        return lax.dot_general(
            metric,
            every,
            (((1,), (0,)), ((), ())),
            precision=lax.Precision.HIGH,
            preferred_element_type=F32,
        )

    def send(fitted):
        chosen = fitted[None, :, :width]
        for o in range(1, occ_count):
            chosen = jnp.where(
                (wanted == o)[:, None, None], fitted[None, :, o * width : (o + 1) * width], chosen
            )
        return lax.all_to_all(chosen, "orb", 0, 0, tiled=True)

    def collect(part):
        arrived = lax.all_to_all(part, "orb", 0, 0, tiled=True)
        return [
            jnp.sum(jnp.where((wanted == o)[:, None, None], arrived, 0.0), axis=0)
            for o in range(occ_count)
        ]

    def total(part, turn):
        members = [(k + turn) % aux_count for k in range(aux_count)]
        return lax.psum(part, "aux", axis_index_groups=[members])

    together = lax.optimization_barrier
    every0, every1 = gather(0), gather(1)
    half0 = send(fit(every0))
    part = first_couplings(slots, half0)
    every1, part = together((every1, part))
    corner = total(part, 0)
    half1 = send(fit(every1))
    mixed, last = rest_couplings(slots, half0, half1)
    mixed, corner = together((mixed, corner))
    mixed = total(mixed, 1)
    last, mixed = together((last, mixed))
    last = total(last, 2)
    out0 = collect(gradient_half(0, slots, shift, vir_energy, half0, half1, corner, mixed))
    out1 = collect(gradient_half(1, slots, shift, vir_energy, half0, half1, last, mixed))
    return jnp.stack(
        [jnp.concatenate([out0[o], out1[o]], axis=1) for o in range(occ_count)], axis=1
    )


def solution(mesh):
    return jax.shard_map(
        body,
        mesh=mesh,
        in_specs=(P("aux", "orb", None), P("aux", None), P(), P(), P()),
        out_specs=P("aux", "orb", None),
        check_vma=False,
    )
```

```python
import functools

import jax
import jax.numpy as jnp
from jax import lax
from jax.experimental import pallas as pl
from jax.experimental.pallas import tpu as pltpu
from jax.sharding import PartitionSpec as P

F32 = jnp.float32
LIMIT = 32 * 1024 * 1024
ROWS = ((0,), (0,))
COLS = ((1,), (1,))
PLAIN = ((1,), (0,))
VMEM = pl.BlockSpec(memory_space=pltpu.VMEM)
SMEM = pl.BlockSpec(memory_space=pltpu.SMEM)
together = lax.optimization_barrier


def split(x):
    high = x.astype(jnp.bfloat16)
    return high, (x - high.astype(F32)).astype(jnp.bfloat16)


def dot3(left, right, dims):
    (lh, ll), (rh, rl) = left, right
    dot = lambda a, b: lax.dot_general(a, b, (dims, ((), ())), preferred_element_type=F32)
    return dot(lh, rh) + (dot(lh, rl) + dot(ll, rh))


def call(kernel, shapes, scalars, arrays, aliases={}):
    return pl.pallas_call(
        kernel,
        in_specs=[SMEM] * len(scalars) + [VMEM] * len(arrays),
        out_specs=[VMEM] * len(shapes),
        out_shape=[jax.ShapeDtypeStruct(s, F32) for s in shapes],
        input_output_aliases=aliases,
        compiler_params=pltpu.CompilerParams(vmem_limit_bytes=LIMIT),
    )(*scalars, *arrays)


def fit_kernel(order, wanted, metric, *refs):
    out, blocks = refs[-1], refs[:-1]
    depth = metric.shape[0]
    width = out.shape[2]
    total = jnp.zeros((depth, blocks[0].shape[1]), F32)
    for k, block in enumerate(blocks):
        place = pl.multiple_of(order[k] * depth, depth)
        total += dot3(split(metric[:, pl.ds(place, depth)]), split(block[...]), PLAIN)
    zero, one = total[:, :width], total[:, width:]
    for t in range(out.shape[0]):

        @pl.when(wanted[t] != 1)
        def _():
            out[t] = zero

        @pl.when(wanted[t] == 1)
        def _():
            out[t] = one


def first_kernel(slots, half, mine, other):
    for k in range(16):
        out = mine if k < 8 else other
        out[k % 8, 0] = dot3(split(half[slots[0, k]]), split(half[slots[1, k]]), ROWS)


def rest_kernel(slots, half0, half1, mixed_mine, mixed_other, last_mine, last_other):
    for k in range(16):
        mixed, last = (mixed_mine, last_mine) if k < 8 else (mixed_other, last_other)
        first, second = slots[0, k], slots[1, k]
        l0, r0 = split(half0[first]), split(half0[second])
        l1, r1 = split(half1[first]), split(half1[second])
        mixed[k % 8, 0] = dot3(l0, r1, ROWS)
        mixed[k % 8, 1] = dot3(l1, r0, ROWS)
        last[k % 8, 0] = dot3(l1, r1, ROWS)


PLACES = [(0, 0), (0, 1), (1, 0), (1, 1), (2, 0), (3, 0), (4, 0), (4, 1)]


def gradient_kernel(fresh, forward_at, back_at, slots, right, left, *refs):
    out, parts = refs[-1], refs[:10]
    out[...] = jnp.zeros_like(out) if fresh else refs[10][...]
    for k in range(16):
        array, at = PLACES[k % 8]
        part = parts[array + (0 if k < 8 else 5)]
        first, second = slots[0, k], slots[1, k]
        forward = split(part[at, forward_at])
        back = forward if forward_at == back_at else split(part[at, back_at])
        out[first] += dot3(split(right[second]), forward, COLS)
        out[second] += dot3(split(left[first]), back, PLAIN)


def body(integrals, metric, occ_energy, vir_energy, pair_orbitals):
    rows, occ_count, vir_count = integrals.shape
    width = vir_count // 2
    orb_count = lax.axis_size("orb")
    my_index = lax.axis_index("orb")
    pair_count = pair_orbitals.shape[0] // orb_count
    pair_ends = pair_orbitals.reshape(orb_count, 2 * pair_count)
    local_pick = jnp.where(pair_ends // occ_count == my_index, pair_ends % occ_count, -1)
    wanted = jnp.max(local_pick, axis=1)
    my_pairs = lax.dynamic_slice_in_dim(pair_orbitals, my_index * pair_count, pair_count, 0)

    my_aux = lax.axis_index("aux")
    my_y, my_core = my_aux // 2, my_aux % 2
    ring = jnp.arange(4, dtype=jnp.int32)
    away = (jnp.arange(2, dtype=jnp.int32)[:, None] + my_core) % 2
    order = (away * 4 + (ring[None, :] + my_y) % 4)[:, :, None] * 2 + jnp.arange(2)[None, None, :]
    hot = order.reshape(-1)[:, None] == jnp.arange(pair_count, dtype=jnp.int32)[None, :]
    near_pairs = jnp.sum(jnp.where(hot[:, :, None], my_pairs[None], 0), axis=1)
    slots = (near_pairs // occ_count).T
    occ_hot = near_pairs[:2, :, None] == jnp.arange(occ_energy.shape[0], dtype=jnp.int32)
    shift = jnp.sum(jnp.where(occ_hot, occ_energy, 0.0), axis=(1, 2))

    def up(x):
        return lax.ppermute(x, "aux", [(k, (k + 2) % 8) for k in range(8)])

    def down(x):
        return lax.ppermute(x, "aux", [(k, (k + 6) % 8) for k in range(8)])

    def across(x):
        return lax.ppermute(x, "aux", [(k, k ^ 1) for k in range(8)])

    def gather(h):
        own = integrals[:, :, h * width : (h + 1) * width].reshape(rows, occ_count * width)
        below, above = up(own), down(own)
        far_low, far_high = up(below[: rows // 2]), down(above[rows // 2 :])
        far = jnp.concatenate([far_low, far_high], axis=0)
        ours = [own, above, far, below]
        return [b for x in ours for b in (x, across(x))]

    metric_order = ((my_y + ring)[:, None] % 4) * 2 + (my_core + jnp.arange(2, dtype=jnp.int32)[None, :]) % 2
    metric_order = metric_order.reshape(-1)

    def send(blocks):
        (chosen,) = call(
            fit_kernel, [(orb_count, rows, width)], [metric_order, wanted], [metric, *blocks]
        )
        return lax.all_to_all(chosen, "orb", 0, 0, tiled=True)

    def reduce_start(mine, other):
        theirs = across(other)
        a2, b2 = up(mine[4:5] + theirs[4:5]), down(mine[5:6] + theirs[5:6])
        return mine, theirs, a2, b2

    def reduce_end(state):
        mine, theirs, a2, b2 = state
        upward = jnp.concatenate([mine[2:3] + theirs[2:3] + a2, mine[3:4] + theirs[3:4]], 0)
        downward = jnp.concatenate([mine[6:7] + theirs[6:7], mine[7:8] + theirs[7:8] + b2], 0)
        return mine[0:2] + theirs[0:2] + up(upward) + down(downward)

    def amplitude(total, starts):
        parts = []
        for k, (i, j) in enumerate(starts):
            column = vir_energy[i : i + width][None, :, None]
            row = vir_energy[j : j + width][None, None, :]
            parts.append(-total[:, k] / (column + row - shift[:, None, None]))
        return jnp.stack(parts, axis=1)

    def spread_start(own):
        return own, up(own), down(own)

    def spread_end(state):
        own, below, above = state
        far_a, far_b = up(below[0:1]), down(above[1:2])
        ours = [own, above, far_a, far_b, below]
        return ours + [across(x) for x in ours]

    def collect(part):
        arrived = lax.all_to_all(part, "orb", 0, 0, tiled=True)
        return [
            jnp.sum(jnp.where((wanted == o)[:, None, None], arrived, 0.0), axis=0)
            for o in range(occ_count)
        ]

    def gradient(forward_at, back_at, half, amplitudes, start=None):
        kernel = functools.partial(gradient_kernel, start is None, forward_at, back_at)
        more = [] if start is None else [start]
        arrays = [half, half, *amplitudes, *more]
        return call(kernel, [half.shape], [slots], arrays, {13: 0} if more else {})[0]

    eight = (8, 1, width, width)
    sixteen = (8, 2, width, width)
    blocks0 = gather(0)
    blocks1 = gather(1)
    half0 = send(blocks0)
    half1 = send(blocks1)
    mine, other = call(first_kernel, [eight, eight], [slots], [half0])
    total = reduce_end(reduce_start(mine, other))
    corner = spread_end(spread_start(amplitude(total, [(0, 0)])))
    grad0 = gradient(0, 0, half0, corner)
    mixed_mine, mixed_other, last_mine, last_other = call(
        rest_kernel, [sixteen, sixteen, eight, eight], [slots], [half0, half1]
    )
    total = reduce_end(reduce_start(mixed_mine, mixed_other))
    spread = spread_start(amplitude(total, [(0, width), (width, 0)]))
    last_mine, spread = together((last_mine, spread))
    mixed = spread_end(spread)
    total = reduce_end(reduce_start(last_mine, last_other))
    last = spread_end(spread_start(amplitude(total, [(width, width)])))
    grad0 = gradient(0, 1, half1, mixed, grad0)
    out0 = collect(grad0)
    grad1 = gradient(1, 0, half0, mixed)
    grad1 = gradient(0, 0, half1, last, grad1)
    out1 = collect(grad1)
    return jnp.stack(
        [jnp.concatenate([out0[o], out1[o]], axis=1) for o in range(occ_count)], axis=1
    )


def solution(mesh):
    return jax.shard_map(
        body,
        mesh=mesh,
        in_specs=(P("aux", "orb", None), P("aux", None), P(), P(), P()),
        out_specs=P("aux", "orb", None),
        check_vma=False,
    )
```

```python
import functools

import jax
import jax.numpy as jnp
from jax import lax
from jax.experimental import pallas as pl
from jax.experimental.pallas import tpu as pltpu
from jax.sharding import PartitionSpec as P

F32 = jnp.float32
LIMIT = 32 * 1024 * 1024
ROWS = ((0,), (0,))
COLS = ((1,), (1,))
PLAIN = ((1,), (0,))
VMEM = pl.BlockSpec(memory_space=pltpu.VMEM)
SMEM = pl.BlockSpec(memory_space=pltpu.SMEM)
together = lax.optimization_barrier


def split(x):
    high = x.astype(jnp.bfloat16)
    return high, (x - high.astype(F32)).astype(jnp.bfloat16)


def dot3(left, right, dims):
    (lh, ll), (rh, rl) = left, right
    dot = lambda a, b: lax.dot_general(a, b, (dims, ((), ())), preferred_element_type=F32)
    return dot(lh, rh) + (dot(lh, rl) + dot(ll, rh))


def call(kernel, shapes, scalars, arrays, scratch=()):
    return pl.pallas_call(
        kernel,
        in_specs=[SMEM] * len(scalars) + [VMEM] * len(arrays),
        out_specs=[VMEM] * len(shapes),
        out_shape=[jax.ShapeDtypeStruct(s, F32) for s in shapes],
        scratch_shapes=[pltpu.VMEM(s, F32) for s in scratch],
        compiler_params=pltpu.CompilerParams(vmem_limit_bytes=LIMIT),
    )(*scalars, *arrays)


def fit_kernel(order, metric, *refs):
    low, high = refs[-2:]
    blocks = refs[:-2]
    depth = metric.shape[0]
    width = low.shape[2]
    total = jnp.zeros((depth, blocks[0].shape[1]), F32)
    for k, block in enumerate(blocks):
        place = pl.multiple_of(order[k] * depth, depth)
        total += dot3(split(metric[:, pl.ds(place, depth)]), split(block[...]), PLAIN)
    for o in range(2):
        columns = total[:, o * width : (o + 1) * width]
        low[o] = columns[: depth // 2]
        high[o] = columns[depth // 2 :]


def select_kernel(table, own, above, far0, far1, below, *outs):
    sources = [(own, 0, own, 1), (above, 0, above, 1), (far0, 0, far1, 0), (below, 0, below, 1)]
    for d, out in enumerate(outs):
        for s, (zero, i, one, j) in enumerate(sources):
            out[s] = jnp.where(table[d, s] == 1, one[j], zero[i])


def fold_kernel(table, *refs):
    arrived, outs = refs[:4], refs[4:]
    for s in range(4):
        for o in range(2):
            total = jnp.where(table[0, s] == o, arrived[0][s], 0.0)
            for e in range(1, 4):
                total += jnp.where(table[e, s] == o, arrived[e][s], 0.0)
            if s == 2:
                outs[2 + o][0] = total
            else:
                outs[s + (s == 3)][o] = total


def assemble(half, arrived):
    low = half.shape[1] // 2
    for d in range(4):
        for s in range(4):
            half[4 * d + s, :low] = arrived[d][s]
            half[4 * s + d, low:] = arrived[4 + d][s]


def first_kernel(slots, *refs):
    half, mine, other = refs[8:]
    assemble(half, refs[:8])
    for k in range(16):
        out = mine if k < 8 else other
        out[k % 8, 0] = dot3(split(half[slots[0, k]]), split(half[slots[1, k]]), ROWS)


def rest_kernel(slots, half0, *refs):
    half1, mixed_mine, mixed_other, last_mine, last_other = refs[8:]
    assemble(half1, refs[:8])
    for k in range(16):
        mixed, last = (mixed_mine, last_mine) if k < 8 else (mixed_other, last_other)
        first, second = slots[0, k], slots[1, k]
        l0, r0 = split(half0[first]), split(half0[second])
        l1, r1 = split(half1[first]), split(half1[second])
        mixed[k % 8, 0] = dot3(l0, r1, ROWS)
        mixed[k % 8, 1] = dot3(l1, r0, ROWS)
        last[k % 8, 0] = dot3(l1, r1, ROWS)


PLACES = [(0, 0), (0, 1), (1, 0), (1, 1), (2, 0), (3, 0), (4, 0), (4, 1)]


def gradient_sum(total, forward_at, back_at, slots, half, parts):
    for k in range(16):
        array, at = PLACES[k % 8]
        part = parts[array + (0 if k < 8 else 5)]
        first, second = slots[0, k], slots[1, k]
        forward = split(part[at, forward_at])
        back = forward if forward_at == back_at else split(part[at, back_at])
        total[first] += dot3(split(half[second]), forward, COLS)
        total[second] += dot3(split(half[first]), back, PLAIN)


def begin_kernel(forward_at, back_at, slots, half, *refs):
    out = refs[-1]
    out[...] = jnp.zeros_like(out)
    gradient_sum(out, forward_at, back_at, slots, half, refs[:10])


def finish_kernel(forward_at, back_at, slots, half, *refs):
    outs, total = refs[11:19], refs[19]
    total[...] = refs[10][...]
    gradient_sum(total, forward_at, back_at, slots, half, refs[:10])
    low = total.shape[1] // 2
    for d in range(4):
        for s in range(4):
            outs[d][s] = total[4 * d + s, :low]
            outs[4 + d][s] = total[4 * s + d, low:]


def body(integrals, metric, occ_energy, vir_energy, pair_orbitals):
    rows, occ_count, vir_count = integrals.shape
    width = vir_count // 2
    orb_count = lax.axis_size("orb")
    my_index = lax.axis_index("orb")
    my_x, my_z = my_index // 4, my_index % 4
    pair_count = pair_orbitals.shape[0] // orb_count
    pair_ends = pair_orbitals.reshape(orb_count, 2 * pair_count)
    owners = jnp.arange(orb_count, dtype=jnp.int32)[None, :, None]
    picks = jnp.max(
        jnp.where(pair_ends[:, None] // occ_count == owners, pair_ends[:, None] % occ_count, -1), 2
    )
    my_pairs = lax.dynamic_slice_in_dim(pair_orbitals, my_index * pair_count, pair_count, 0)

    def at(table, index, axis):
        hot = index.reshape((-1, 1)) == jnp.arange(table.shape[axis], dtype=jnp.int32)
        hot = hot.reshape((-1,) + (1,) * axis + (table.shape[axis],) + (1,) * (table.ndim - 1 - axis))
        return jnp.moveaxis(jnp.sum(jnp.where(hot, table[None], 0), axis=axis + 1), 0, axis)

    my_aux = lax.axis_index("aux")
    my_y, my_core = my_aux // 2, my_aux % 2
    ring = jnp.arange(4, dtype=jnp.int32)
    away = (jnp.arange(2, dtype=jnp.int32)[:, None] + my_core) % 2
    order = (away * 4 + (ring[None, :] + my_y) % 4)[:, :, None] * 2 + jnp.arange(2)[None, None, :]
    hot = order.reshape(-1)[:, None] == jnp.arange(pair_count, dtype=jnp.int32)[None, :]
    near_pairs = jnp.sum(jnp.where(hot[:, :, None], my_pairs[None], 0), axis=1)
    blocks = near_pairs // occ_count
    slots = ((blocks % 4 - my_z) % 4 * 4 + (blocks // 4 - my_x) % 4).T
    same_z = (my_x + ring) % 4 * 4 + my_z
    same_x = my_x * 4 + (my_z + ring) % 4
    table_low = at(at(picks, same_x, 0), same_z, 1)
    table_high = at(at(picks, same_z, 0), same_x, 1)
    occ_hot = near_pairs[:2, :, None] == jnp.arange(occ_energy.shape[0], dtype=jnp.int32)
    shift = jnp.sum(jnp.where(occ_hot, occ_energy, 0.0), axis=(1, 2))

    def up(x):
        return lax.ppermute(x, "aux", [(k, (k + 2) % 8) for k in range(8)])

    def down(x):
        return lax.ppermute(x, "aux", [(k, (k + 6) % 8) for k in range(8)])

    def across(x):
        return lax.ppermute(x, "aux", [(k, k ^ 1) for k in range(8)])

    def move(dx, dz):
        perm = [(x * 4 + z, (x + dx) % 4 * 4 + (z + dz) % 4) for x in range(4) for z in range(4)]
        return lambda a: lax.ppermute(a, "orb", perm)

    along_x = move(1, 0), move(3, 0), move(2, 0)
    along_z = move(0, 1), move(0, 3), move(0, 2)

    def gather(h):
        own = integrals[:, :, h * width : (h + 1) * width].reshape(rows, occ_count * width)
        below, above = up(own), down(own)
        far_low, far_high = up(below[: rows // 2]), down(above[rows // 2 :])
        far = jnp.concatenate([far_low, far_high], axis=0)
        ours = [own, above, far, below]
        return [b for x in ours for b in (x, across(x))]

    cores = jnp.arange(2, dtype=jnp.int32)[None, :]
    metric_order = (((my_y + ring)[:, None] % 4) * 2 + (my_core + cores) % 2).reshape(-1)
    strip = (2, rows // 2, width)
    piece = (4, rows // 2, width)

    def ring_gather(own, moves):
        forth, back, _ = moves
        below, above = forth(own), back(own)
        return own, above, forth(below[0:1]), back(above[1:2]), below

    def exchange(parts, moves):
        forth, back, across_ring = moves
        return [parts[0], back(parts[3]), across_ring(parts[2]), forth(parts[1])]

    def send(blocks):
        low, high = call(fit_kernel, [strip, strip], [metric_order], [metric, *blocks])
        near_low, near_high = ring_gather(low, along_x), ring_gather(high, along_z)
        low = call(select_kernel, [piece] * 4, [table_low], near_low)
        high = call(select_kernel, [piece] * 4, [table_high], near_high)
        return exchange(low, along_z) + exchange(high, along_x)

    def ring_reduce(parts, moves):
        forth, back, _ = moves
        own, next_, far0, far1, last = parts
        far0, far1 = forth(far0), back(far1)
        upward = jnp.concatenate([next_[0:1] + far0, next_[1:2]], 0)
        downward = jnp.concatenate([last[0:1], last[1:2] + far1], 0)
        return own + forth(upward) + back(downward)

    def collect(parts):
        folded = [strip, strip, (1, *strip[1:]), (1, *strip[1:]), strip]
        low, high = exchange(parts[:4], along_z), exchange(parts[4:], along_x)
        low = call(fold_kernel, folded, [table_low], low)
        high = call(fold_kernel, folded, [table_high], high)
        return jnp.concatenate([ring_reduce(low, along_x), ring_reduce(high, along_z)], axis=1)

    def reduce_start(mine, other):
        theirs = across(other)
        a2, b2 = up(mine[4:5] + theirs[4:5]), down(mine[5:6] + theirs[5:6])
        return mine, theirs, a2, b2

    def reduce_end(state):
        mine, theirs, a2, b2 = state
        upward = jnp.concatenate([mine[2:3] + theirs[2:3] + a2, mine[3:4] + theirs[3:4]], 0)
        downward = jnp.concatenate([mine[6:7] + theirs[6:7], mine[7:8] + theirs[7:8] + b2], 0)
        return mine[0:2] + theirs[0:2] + up(upward) + down(downward)

    def amplitude(total, starts):
        parts = []
        for k, (i, j) in enumerate(starts):
            column = vir_energy[i : i + width][None, :, None]
            row = vir_energy[j : j + width][None, None, :]
            parts.append(-total[:, k] / (column + row - shift[:, None, None]))
        return jnp.stack(parts, axis=1)

    def spread_start(own):
        return own, up(own), down(own)

    def spread_end(state):
        own, below, above = state
        far_a, far_b = up(below[0:1]), down(above[1:2])
        ours = [own, above, far_a, far_b, below]
        return ours + [across(x) for x in ours]

    def begin(forward_at, back_at, half, amplitudes, slots):
        kernel = functools.partial(begin_kernel, forward_at, back_at)
        return call(kernel, [half.shape], [slots], [half, *amplitudes])[0]

    def finish(forward_at, back_at, half, amplitudes, start):
        kernel = functools.partial(finish_kernel, forward_at, back_at)
        return call(kernel, [piece] * 8, [slots], [half, *amplitudes, start], [half.shape])

    eight = (8, 1, width, width)
    sixteen = (8, 2, width, width)
    whole = (orb_count, rows, width)
    blocks0, blocks1 = gather(0), gather(1)
    half0, mine, other = call(first_kernel, [whole, eight, eight], [slots], send(blocks0))
    pieces1 = send(blocks1)
    total = reduce_end(reduce_start(mine, other))
    spread = spread_start(amplitude(total, [(0, 0)]))
    pieces1, spread = together((pieces1, spread))
    corner = spread_end(spread)
    half1, mixed_mine, mixed_other, last_mine, last_other = call(
        rest_kernel, [whole, sixteen, sixteen, eight, eight], [slots], [half0, *pieces1]
    )
    grad0 = begin(0, 0, half0, corner, slots)
    state = reduce_start(mixed_mine, mixed_other)
    state, grad0 = together((state, grad0))
    total = reduce_end(state)
    spread = spread_start(amplitude(total, [(0, width), (width, 0)]))
    last_mine, spread = together((last_mine, spread))
    mixed = spread_end(spread)
    grad0 = finish(0, 1, half1, mixed, grad0)
    later_slots, grad0 = together((slots, grad0))
    grad1 = begin(1, 0, half0, mixed, later_slots)
    total = reduce_end(reduce_start(last_mine, last_other))
    spread = spread_start(amplitude(total, [(width, width)]))
    spread, grad1 = together((spread, grad1))
    last = spread_end(spread)
    out0 = collect(grad0)
    out1 = collect(finish(0, 0, half1, last, grad1))
    return jnp.concatenate([out0, out1], axis=2).transpose(1, 0, 2)


def solution(mesh):
    return jax.shard_map(
        body,
        mesh=mesh,
        in_specs=(P("aux", "orb", None), P("aux", None), P(), P(), P()),
        out_specs=P("aux", "orb", None),
        check_vma=False,
    )
```

```python
import functools

import jax
import jax.numpy as jnp
from jax import lax
from jax.experimental import pallas as pl
from jax.experimental.pallas import tpu as pltpu
from jax.sharding import PartitionSpec as P

F32 = jnp.float32
LIMIT = 32 * 1024 * 1024
ROWS = ((0,), (0,))
COLS = ((1,), (1,))
PLAIN = ((1,), (0,))
VMEM = pl.BlockSpec(memory_space=pltpu.VMEM)
SMEM = pl.BlockSpec(memory_space=pltpu.SMEM)
together = lax.optimization_barrier


def split(x):
    high = x.astype(jnp.bfloat16)
    return high, (x - high.astype(F32)).astype(jnp.bfloat16)


def dot3(left, right, dims):
    (lh, ll), (rh, rl) = left, right
    dot = lambda a, b: lax.dot_general(a, b, (dims, ((), ())), preferred_element_type=F32)
    return dot(lh, rh) + (dot(lh, rl) + dot(ll, rh))


def call(kernel, shapes, scalars, arrays, scratch=()):
    return pl.pallas_call(
        kernel,
        in_specs=[SMEM] * len(scalars) + [VMEM] * len(arrays),
        out_specs=[VMEM] * len(shapes),
        out_shape=[jax.ShapeDtypeStruct(s, F32) for s in shapes],
        scratch_shapes=[pltpu.VMEM(s, F32) for s in scratch],
        compiler_params=pltpu.CompilerParams(vmem_limit_bytes=LIMIT),
    )(*scalars, *arrays)


def strips(total, low, high):
    half, width = low.shape[1:]
    for o in range(2):
        columns = total[:, o * width : (o + 1) * width]
        low[o] = columns[:half]
        high[o] = columns[half:]


def fit_kernel(order, metric, *refs):
    blocks = refs[:-2]
    depth = metric.shape[0]
    total = jnp.zeros((depth, blocks[0].shape[1]), F32)
    for k, block in enumerate(blocks):
        place = pl.multiple_of(order[k] * depth, depth)
        total += dot3(split(metric[:, pl.ds(place, depth)]), split(block[...]), PLAIN)
    strips(total, *refs[-2:])


def fit_whole_kernel(metric, every, low, high):
    depth = metric.shape[0]
    total = jnp.zeros((depth, every.shape[1]), F32)
    for k in range(metric.shape[1] // depth):
        block = slice(k * depth, (k + 1) * depth)
        total += dot3(split(metric[:, block]), split(every[block]), PLAIN)
    strips(total, low, high)


def select_kernel(tables, *refs):
    arrived, outs = refs[:8], refs[8:]
    for side in range(2):
        for d in range(4):
            for s in range(4):
                block = arrived[4 * side + s]
                outs[4 * side + d][s] = jnp.where(tables[side, d, s] == 1, block[1], block[0])


def fold_kernel(tables, *refs):
    arrived, outs = refs[:8], refs[8:]
    for side in range(2):
        for s in range(4):
            for o in range(2):
                total = jnp.where(tables[side, 0, s] == o, arrived[4 * side][s], 0.0)
                for e in range(1, 4):
                    total += jnp.where(tables[side, e, s] == o, arrived[4 * side + e][s], 0.0)
                outs[4 * side + s][o] = total


def assemble(half, arrived):
    low = half.shape[1] // 2
    for d in range(4):
        for s in range(4):
            half[4 * d + s, :low] = arrived[d][s]
            half[4 * s + d, low:] = arrived[4 + d][s]


def first_kernel(slots, *refs):
    half, mine, other = refs[8:]
    assemble(half, refs[:8])
    for k in range(16):
        out = mine if k < 8 else other
        out[k % 8, 0] = dot3(split(half[slots[0, k]]), split(half[slots[1, k]]), ROWS)


def mixed_couplings(slots, half0, half1, out, start):
    for k in range(8):
        first, second = slots[0, start + k], slots[1, start + k]
        out[k, 0] = dot3(split(half0[first]), split(half1[second]), ROWS)
        out[k, 1] = dot3(split(half1[first]), split(half0[second]), ROWS)


def mixed_other_kernel(slots, half0, *refs):
    half1, out = refs[8:]
    assemble(half1, refs[:8])
    mixed_couplings(slots, half0, half1, out, 8)


def mixed_mine_kernel(slots, half0, half1, out):
    mixed_couplings(slots, half0, half1, out, 0)


def last_kernel(slots, half, mine, other):
    for k in range(16):
        out = mine if k < 8 else other
        out[k % 8, 0] = dot3(split(half[slots[0, k]]), split(half[slots[1, k]]), ROWS)


PLACES = [(0, 0), (0, 1), (1, 0), (1, 1), (2, 0), (2, 1), (1, 2), (1, 3)]


def gradient_sum(total, forward_at, back_at, slots, half, parts):
    for k in range(16):
        array, at = PLACES[k % 8]
        part = parts[array + (0 if k < 8 else 3)]
        first, second = slots[0, k], slots[1, k]
        forward = split(part[at, forward_at])
        back = forward if forward_at == back_at else split(part[at, back_at])
        total[first] += dot3(split(half[second]), forward, COLS)
        total[second] += dot3(split(half[first]), back, PLAIN)


def begin_kernel(forward_at, back_at, slots, half, *refs):
    out = refs[-1]
    out[...] = jnp.zeros_like(out)
    gradient_sum(out, forward_at, back_at, slots, half, refs[:6])


def finish_kernel(forward_at, back_at, slots, half, *refs):
    outs, total = refs[7:15], refs[15]
    total[...] = refs[6][...]
    gradient_sum(total, forward_at, back_at, slots, half, refs[:6])
    low = total.shape[1] // 2
    for d in range(4):
        for s in range(4):
            outs[d][s] = total[4 * d + s, :low]
            outs[4 + d][s] = total[4 * s + d, low:]


def body(integrals, metric, occ_energy, vir_energy, pair_orbitals):
    rows, occ_count, vir_count = integrals.shape
    width = vir_count // 2
    orb_count = lax.axis_size("orb")
    my_index = lax.axis_index("orb")
    my_x, my_z = my_index // 4, my_index % 4
    pair_count = pair_orbitals.shape[0] // orb_count
    pair_ends = pair_orbitals.reshape(orb_count, 2 * pair_count)
    owners = jnp.arange(orb_count, dtype=jnp.int32)[None, :, None]
    picks = jnp.max(
        jnp.where(pair_ends[:, None] // occ_count == owners, pair_ends[:, None] % occ_count, -1), 2
    )
    my_pairs = lax.dynamic_slice_in_dim(pair_orbitals, my_index * pair_count, pair_count, 0)

    def at(table, index, axis):
        hot = index.reshape((-1, 1)) == jnp.arange(table.shape[axis], dtype=jnp.int32)
        hot = hot.reshape((-1,) + (1,) * axis + (table.shape[axis],) + (1,) * (table.ndim - 1 - axis))
        return jnp.moveaxis(jnp.sum(jnp.where(hot, table[None], 0), axis=axis + 1), 0, axis)

    my_aux = lax.axis_index("aux")
    my_y, my_core = my_aux // 2, my_aux % 2
    ring = jnp.arange(4, dtype=jnp.int32)
    away = (jnp.arange(2, dtype=jnp.int32)[:, None] + my_core) % 2
    order = (away * 4 + (ring[None, :] + my_y) % 4)[:, :, None] * 2 + jnp.arange(2)[None, None, :]
    hot = order.reshape(-1)[:, None] == jnp.arange(pair_count, dtype=jnp.int32)[None, :]
    near_pairs = jnp.sum(jnp.where(hot[:, :, None], my_pairs[None], 0), axis=1)
    blocks = near_pairs // occ_count
    slots = ((blocks % 4 - my_z) % 4 * 4 + (blocks // 4 - my_x) % 4).T
    same_z = (my_x + ring) % 4 * 4 + my_z
    same_x = my_x * 4 + (my_z + ring) % 4
    tables = jnp.stack(
        [at(at(picks, same_x, 0), same_z, 1), at(at(picks, same_z, 0), same_x, 1)]
    )
    occ_hot = near_pairs[:2, :, None] == jnp.arange(occ_energy.shape[0], dtype=jnp.int32)
    shift = jnp.sum(jnp.where(occ_hot, occ_energy, 0.0), axis=(1, 2))

    def up(x):
        return lax.ppermute(x, "aux", [(k, (k + 2) % 8) for k in range(8)])

    def down(x):
        return lax.ppermute(x, "aux", [(k, (k + 6) % 8) for k in range(8)])

    def across(x):
        return lax.ppermute(x, "aux", [(k, k ^ 1) for k in range(8)])

    def move(dx, dz):
        perm = [(x * 4 + z, (x + dx) % 4 * 4 + (z + dz) % 4) for x in range(4) for z in range(4)]
        return lambda a: lax.ppermute(a, "orb", perm)

    along_x = move(1, 0), move(3, 0), move(2, 0)
    along_z = move(0, 1), move(0, 3), move(0, 2)

    def part_of(h):
        return integrals[:, :, h * width : (h + 1) * width].reshape(rows, occ_count * width)

    cores = jnp.arange(2, dtype=jnp.int32)[None, :]
    metric_order = (((my_y + ring)[:, None] % 4) * 2 + (my_core + cores) % 2).reshape(-1)
    strip = (2, rows // 2, width)
    piece = (4, rows // 2, width)

    def exchange(parts, moves):
        forth, back, across_ring = moves
        return [parts[0], back(parts[3]), across_ring(parts[2]), forth(parts[1])]

    def send(fitted):
        low, high = fitted
        arrived = exchange([low] * 4, along_x) + exchange([high] * 4, along_z)
        chosen = call(select_kernel, [piece] * 8, [tables], arrived)
        return exchange(chosen[:4], along_z) + exchange(chosen[4:], along_x)

    def collect(parts):
        arrived = exchange(parts[:4], along_z) + exchange(parts[4:], along_x)
        sums = call(fold_kernel, [strip] * 8, [tables], arrived)
        low, high = exchange(sums[:4], along_x), exchange(sums[4:], along_z)
        return jnp.concatenate([sum(low[1:], low[0]), sum(high[1:], high[0])], axis=1)

    def reduce_start(mine, other):
        theirs = across(other)
        a2, b2 = up(mine[4:5] + theirs[4:5]), down(mine[5:6] + theirs[5:6])
        return mine, theirs, a2, b2

    def reduce_end(state):
        mine, theirs, a2, b2 = state
        upward = jnp.concatenate([mine[2:3] + theirs[2:3] + a2, mine[3:4] + theirs[3:4]], 0)
        downward = jnp.concatenate([mine[6:7] + theirs[6:7], mine[7:8] + theirs[7:8] + b2], 0)
        return mine[0:2] + theirs[0:2] + up(upward) + down(downward)

    def amplitude(total, starts):
        parts = []
        for k, (i, j) in enumerate(starts):
            column = vir_energy[i : i + width][None, :, None]
            row = vir_energy[j : j + width][None, None, :]
            parts.append(-total[:, k] / (column + row - shift[:, None, None]))
        return jnp.stack(parts, axis=1)

    def spread_start(own):
        return own, up(own), down(own)

    def spread_far(state):
        own, below, above = state
        far = jnp.concatenate([up(below[0:1]), down(above[1:2])], 0)
        return [own, jnp.concatenate([above, below], 0), far]

    def spread_end(ours):
        return list(ours) + [across(x) for x in ours]

    def begin(forward_at, back_at, half, amplitudes, slots):
        kernel = functools.partial(begin_kernel, forward_at, back_at)
        return call(kernel, [half.shape], [slots], [half, *amplitudes])[0]

    def finish(forward_at, back_at, half, amplitudes, start):
        kernel = functools.partial(finish_kernel, forward_at, back_at)
        return call(kernel, [piece] * 8, [slots], [half, *amplitudes, start], [half.shape])

    eight = (8, 1, width, width)
    sixteen = (8, 2, width, width)
    whole = (orb_count, rows, width)
    own = part_of(0)
    below, above = up(own), down(own)
    far = jnp.concatenate([up(below[: rows // 2]), down(above[rows // 2 :])], axis=0)
    blocks = [b for x in (own, above, far, below) for b in (x, across(x))]
    later, far = together((part_of(1), far))
    every = lax.all_gather(later, "aux", axis=0, tiled=True)
    pieces0 = send(call(fit_kernel, [strip, strip], [metric_order], [metric, *blocks]))
    every, pieces0 = together((every, pieces0))
    fitted1 = call(fit_whole_kernel, [strip, strip], [], [metric, every])
    half0, mine, other = call(first_kernel, [whole, eight, eight], [slots], pieces0)
    pieces1 = send(fitted1)
    total = reduce_end(reduce_start(mine, other))
    corner = spread_far(spread_start(amplitude(total, [(0, 0)])))
    pieces1, corner = together((pieces1, corner))
    half1, mixed_other = call(mixed_other_kernel, [whole, sixteen], [slots], [half0, *pieces1])
    (mixed_mine,) = call(mixed_mine_kernel, [sixteen], [slots], [half0, half1])
    state = reduce_start(mixed_mine, mixed_other)
    state, corner, late_half1 = together((state, corner, half1))
    last_mine, last_other = call(last_kernel, [eight, eight], [slots], [late_half1])
    total = reduce_end(state)
    spread = spread_start(amplitude(total, [(0, width), (width, 0)]))
    grad0 = begin(0, 0, half0, spread_end(corner), slots)
    spread, grad0 = together((spread, grad0))
    mixed = spread_far(spread)
    last_mine, mixed = together((last_mine, mixed))
    mixed = spread_end(mixed)
    grad0 = finish(0, 1, half1, mixed, grad0)
    later_slots, grad0 = together((slots, grad0))
    grad1 = begin(1, 0, half0, mixed, later_slots)
    total = reduce_end(reduce_start(last_mine, last_other))
    spread = spread_start(amplitude(total, [(width, width)]))
    spread, grad1 = together((spread, grad1))
    last = spread_end(spread_far(spread))
    out0 = collect(grad0)
    out1 = collect(finish(0, 0, half1, last, grad1))
    return jnp.concatenate([out0, out1], axis=2).transpose(1, 0, 2)


def solution(mesh):
    return jax.shard_map(
        body,
        mesh=mesh,
        in_specs=(P("aux", "orb", None), P("aux", None), P(), P(), P()),
        out_specs=P("aux", "orb", None),
        check_vma=False,
    )
```

```python
import functools

import jax
import jax.numpy as jnp
from jax import lax
from jax.experimental import pallas as pl
from jax.experimental.pallas import tpu as pltpu
from jax.sharding import PartitionSpec as P

F32 = jnp.float32
LIMIT = 16 * 1024 * 1024
ROWS = ((0,), (0,))
COLS = ((1,), (1,))
PLAIN = ((1,), (0,))
VMEM = pl.BlockSpec(memory_space=pltpu.VMEM)
SMEM = pl.BlockSpec(memory_space=pltpu.SMEM)
together = lax.optimization_barrier


def split(x):
    high = x.astype(jnp.bfloat16)
    return high, (x - high.astype(F32)).astype(jnp.bfloat16)


def dot3(left, right, dims):
    (lh, ll), (rh, rl) = left, right
    dot = lambda a, b: lax.dot_general(a, b, (dims, ((), ())), preferred_element_type=F32)
    return dot(lh, rh) + (dot(lh, rl) + dot(ll, rh))


def call(kernel, shapes, scalars, arrays, scratch=()):
    return pl.pallas_call(
        kernel,
        in_specs=[SMEM] * len(scalars) + [VMEM] * len(arrays),
        out_specs=[VMEM] * len(shapes),
        out_shape=[jax.ShapeDtypeStruct(s, F32) for s in shapes],
        scratch_shapes=[pltpu.VMEM(s, F32) for s in scratch],
        compiler_params=pltpu.CompilerParams(vmem_limit_bytes=LIMIT),
    )(*scalars, *arrays)


def place_fitted(total, out):
    width = out.shape[2]
    for o in range(2):
        out[o] = total[:, o * width : (o + 1) * width]


def fit_kernel(order, metric, *refs):
    blocks, out = refs[:-1], refs[-1]
    depth = metric.shape[0]
    total = jnp.zeros((depth, blocks[0].shape[1]), F32)
    for k, block in enumerate(blocks):
        place = pl.multiple_of(order[k] * depth, depth)
        total += dot3(split(metric[:, pl.ds(place, depth)]), split(block[...]), PLAIN)
    place_fitted(total, out)


def fit_whole_kernel(metric, every, out):
    depth = metric.shape[0]
    total = jnp.zeros((depth, every.shape[1]), F32)
    for k in range(metric.shape[1] // depth):
        block = slice(k * depth, (k + 1) * depth)
        total += dot3(split(metric[:, block]), split(every[block]), PLAIN)
    place_fitted(total, out)


def select_kernel(table, *refs):
    blocks, outs = refs[:4], refs[4:]
    for d in range(4):
        for s in range(4):
            outs[d][s] = jnp.where(table[d, s] == 1, blocks[s][1], blocks[s][0])


def fold_kernel(table, *refs):
    arrived, outs = refs[:4], refs[4:]
    for s in range(4):
        for o in range(2):
            total = jnp.where(table[0, s] == o, arrived[0][s], 0.0)
            for e in range(1, 4):
                total += jnp.where(table[e, s] == o, arrived[e][s], 0.0)
            outs[s][o] = total


def assemble(half, arrived):
    for d in range(4):
        half[4 * d : 4 * d + 4] = arrived[d][...]


def corner_couplings(slots, half, mine, other):
    for k in range(16):
        out = mine if k < 8 else other
        out[k % 8, 0] = dot3(split(half[slots[0, k]]), split(half[slots[1, k]]), ROWS)


def corner_kernel(slots, half, mine, other):
    corner_couplings(slots, half, mine, other)


def assembled_corner_kernel(slots, *refs):
    half, mine, other = refs[4:]
    assemble(half, refs[:4])
    corner_couplings(slots, half, mine, other)


def mixed_couplings(slots, half0, half1, out, start):
    for k in range(8):
        first, second = slots[0, start + k], slots[1, start + k]
        out[k, 0] = dot3(split(half0[first]), split(half1[second]), ROWS)
        out[k, 1] = dot3(split(half1[first]), split(half0[second]), ROWS)


def mixed_kernel(slots, half0, half1, out):
    mixed_couplings(slots, half0, half1, out, 0)


def assembled_mixed_kernel(slots, half0, *refs):
    half1, out = refs[4:]
    assemble(half1, refs[:4])
    mixed_couplings(slots, half0, half1, out, 8)


PLACES = [(0, 0), (0, 1), (1, 0), (1, 1), (2, 0), (2, 1), (1, 2), (1, 3)]


def gradient_sum(total, forward_at, back_at, slots, half, parts):
    for k in range(16):
        array, at = PLACES[k % 8]
        part = parts[array + (0 if k < 8 else 3)]
        first, second = slots[0, k], slots[1, k]
        forward = split(part[at, forward_at])
        back = forward if forward_at == back_at else split(part[at, back_at])
        total[first] += dot3(split(half[second]), forward, COLS)
        total[second] += dot3(split(half[first]), back, PLAIN)


def begin_kernel(forward_at, back_at, slots, half, *refs):
    out = refs[-1]
    out[...] = jnp.zeros_like(out)
    gradient_sum(out, forward_at, back_at, slots, half, refs[:6])


def finish_kernel(forward_at, back_at, slots, half, *refs):
    outs, total = refs[7:-1], refs[-1]
    total[...] = refs[6][...]
    gradient_sum(total, forward_at, back_at, slots, half, refs[:6])
    for d in range(4):
        outs[d][...] = total[4 * d : 4 * d + 4]


def body(integrals, metric, occ_energy, vir_energy, pair_orbitals):
    rows, occ_count, vir_count = integrals.shape
    width = vir_count // 2
    orb_count = lax.axis_size("orb")
    my_index = lax.axis_index("orb")
    my_x, my_z = my_index // 4, my_index % 4
    pair_count = pair_orbitals.shape[0] // orb_count
    pair_ends = pair_orbitals.reshape(orb_count, 2 * pair_count)
    owners = jnp.arange(orb_count, dtype=jnp.int32)[None, :, None]
    picks = jnp.max(
        jnp.where(pair_ends[:, None] // occ_count == owners, pair_ends[:, None] % occ_count, -1), 2
    )
    my_pairs = lax.dynamic_slice_in_dim(pair_orbitals, my_index * pair_count, pair_count, 0)

    def at(table, index, axis):
        hot = index.reshape((-1, 1)) == jnp.arange(table.shape[axis], dtype=jnp.int32)
        hot = hot.reshape((-1,) + (1,) * axis + (table.shape[axis],) + (1,) * (table.ndim - 1 - axis))
        return jnp.moveaxis(jnp.sum(jnp.where(hot, table[None], 0), axis=axis + 1), 0, axis)

    my_aux = lax.axis_index("aux")
    my_y, my_core = my_aux // 2, my_aux % 2
    ring = jnp.arange(4, dtype=jnp.int32)
    away = (jnp.arange(2, dtype=jnp.int32)[:, None] + my_core) % 2
    order = (away * 4 + (ring[None, :] + my_y) % 4)[:, :, None] * 2 + jnp.arange(2)[None, None, :]
    hot = order.reshape(-1)[:, None] == jnp.arange(pair_count, dtype=jnp.int32)[None, :]
    near_pairs = jnp.sum(jnp.where(hot[:, :, None], my_pairs[None], 0), axis=1)
    blocks = near_pairs // occ_count
    away_x, away_z = (blocks // 4 - my_x) % 4, (blocks % 4 - my_z) % 4
    slots = jnp.where(my_core == 0, away_z * 4 + away_x, away_x * 4 + away_z).T
    same_z = (my_x + ring) % 4 * 4 + my_z
    same_x = my_x * 4 + (my_z + ring) % 4
    near = jnp.where(my_core == 0, same_z, same_x)
    table = at(at(picks, jnp.where(my_core == 0, same_x, same_z), 0), near, 1)
    occ_hot = near_pairs[:2, :, None] == jnp.arange(occ_energy.shape[0], dtype=jnp.int32)
    shift = jnp.sum(jnp.where(occ_hot, occ_energy, 0.0), axis=(1, 2))

    def up(x):
        return lax.ppermute(x, "aux", [(k, (k + 2) % 8) for k in range(8)])

    def down(x):
        return lax.ppermute(x, "aux", [(k, (k + 6) % 8) for k in range(8)])

    def across(x):
        return lax.ppermute(x, "aux", [(k, k ^ 1) for k in range(8)])

    def move(step, by_x):
        perm = []
        for a in range(8):
            for x in range(4):
                for z in range(4):
                    if a % 2 == by_x:
                        to = (x + step) % 4 * 4 + z
                    else:
                        to = x * 4 + (z + step) % 4
                    perm.append((a * 16 + x * 4 + z, a * 16 + to))
        return lambda v: lax.ppermute(v, ("aux", "orb"), perm)

    near_moves = move(1, 0), move(3, 0), move(2, 0)
    far_moves = move(1, 1), move(3, 1), move(2, 1)

    def part_of(h):
        return integrals[:, :, h * width : (h + 1) * width].reshape(rows, occ_count * width)

    cores = jnp.arange(2, dtype=jnp.int32)[None, :]
    metric_order = (((my_y + ring)[:, None] % 4) * 2 + (my_core + cores) % 2).reshape(-1)
    strip = (2, rows, width)
    piece = (4, rows, width)

    def exchange(parts, moves):
        forth, back, across_ring = moves
        return [parts[0], back(parts[3]), across_ring(parts[2]), forth(parts[1])]

    def send(fitted, beside):
        arrived = exchange([fitted] * 4, near_moves)
        chosen = call(select_kernel, [piece] * 4, [table], arrived)
        chosen, beside = together((chosen, beside))
        return exchange(chosen, far_moves), beside

    def collect(parts):
        sums = call(fold_kernel, [strip] * 4, [table], exchange(parts, far_moves))
        sums = exchange(sums, near_moves)
        return sum(sums[1:], sums[0])

    def reduce_start(mine, other):
        theirs = across(other)
        a2, b2 = up(mine[4:5] + theirs[4:5]), down(mine[5:6] + theirs[5:6])
        return mine, theirs, a2, b2

    def reduce_end(state):
        mine, theirs, a2, b2 = state
        upward = jnp.concatenate([mine[2:3] + theirs[2:3] + a2, mine[3:4] + theirs[3:4]], 0)
        downward = jnp.concatenate([mine[6:7] + theirs[6:7], mine[7:8] + theirs[7:8] + b2], 0)
        return mine[0:2] + theirs[0:2] + up(upward) + down(downward)

    def amplitude(total, starts):
        parts = []
        for k, (i, j) in enumerate(starts):
            column = vir_energy[i : i + width][None, :, None]
            row = vir_energy[j : j + width][None, None, :]
            parts.append(-total[:, k] / (column + row - shift[:, None, None]))
        return jnp.stack(parts, axis=1)

    def spread_start(own):
        return own, up(own), down(own)

    def spread_far(state):
        own, below, above = state
        far = jnp.concatenate([up(below[0:1]), down(above[1:2])], 0)
        return [own, jnp.concatenate([above, below], 0), far]

    def spread_end(ours):
        return list(ours) + [across(x) for x in ours]

    def begin(forward_at, back_at, half, amplitudes, slots):
        kernel = functools.partial(begin_kernel, forward_at, back_at)
        return call(kernel, [whole], [slots], [half, *amplitudes])[0]

    def finish(forward_at, back_at, half, amplitudes, start):
        kernel = functools.partial(finish_kernel, forward_at, back_at)
        return call(kernel, [piece] * 4, [slots], [half, *amplitudes, start], [whole])

    eight = (8, 1, width, width)
    sixteen = (8, 2, width, width)
    whole = (orb_count, rows, width)
    own = part_of(0)
    below, above = up(own), down(own)
    far = jnp.concatenate([up(below[: rows // 2]), down(above[rows // 2 :])], axis=0)
    blocks = [b for x in (own, above, far, below) for b in (x, across(x))]
    later, far = together((part_of(1), far))
    every = lax.all_gather(later, "aux", axis=0, tiled=True)
    (fitted,) = call(fit_kernel, [strip], [metric_order], [metric, *blocks])
    arrived, every = send(fitted, every)
    (fitted,) = call(fit_whole_kernel, [strip], [], [metric, every])
    fitted, arrived = together((fitted, arrived))
    half0, mine, other = call(assembled_corner_kernel, [whole, eight, eight], [slots], arrived)
    arrived, _ = send(fitted, ())
    total = reduce_end(reduce_start(mine, other))
    corner = spread_far(spread_start(amplitude(total, [(0, 0)])))
    arrived, corner = together((arrived, corner))
    half1, other = call(assembled_mixed_kernel, [whole, sixteen], [slots], [half0, *arrived])
    (mine,) = call(mixed_kernel, [sixteen], [slots], [half0, half1])
    state = reduce_start(mine, other)
    state, corner, late_half1 = together((state, corner, half1))
    mine, other = call(corner_kernel, [eight, eight], [slots], [late_half1])
    total = reduce_end(state)
    spread = spread_start(amplitude(total, [(0, width), (width, 0)]))
    grad0 = begin(0, 0, half0, spread_end(corner), slots)
    spread, grad0, mine, other = together((spread, grad0, mine, other))
    mixed = spread_far(spread)
    mine, mixed[2] = together((mine, mixed[2]))
    mixed = spread_end(mixed)
    grad0 = finish(0, 1, half1, mixed, grad0)
    state = reduce_start(mine, other)
    later_slots, state, grad0 = together((slots, state, grad0))
    grad1 = begin(1, 0, half0, mixed, later_slots)
    spread = spread_start(amplitude(reduce_end(state), [(width, width)]))
    spread, grad1 = together((spread, grad1))
    last = spread_end(spread_far(spread))
    first = collect(grad0)
    second = collect(finish(0, 0, half1, last, grad1))
    return jnp.concatenate([first, second], axis=2).transpose(1, 0, 2)


def solution(mesh):
    return jax.shard_map(
        body,
        mesh=mesh,
        in_specs=(P("aux", "orb", None), P("aux", None), P(), P(), P()),
        out_specs=P("aux", "orb", None),
        check_vma=False,
    )
```

```python
import functools

import jax
import jax.numpy as jnp
from jax import lax
from jax.experimental import pallas as pl
from jax.experimental.pallas import tpu as pltpu
from jax.sharding import PartitionSpec as P

F32 = jnp.float32
LIMIT = 16 * 1024 * 1024
ROWS = ((0,), (0,))
COLS = ((1,), (1,))
PLAIN = ((1,), (0,))
VMEM = pl.BlockSpec(memory_space=pltpu.VMEM)
SMEM = pl.BlockSpec(memory_space=pltpu.SMEM)
together = lax.optimization_barrier


def split(x):
    high = x.astype(jnp.bfloat16)
    return high, (x - high.astype(F32)).astype(jnp.bfloat16)


def dot3(left, right, dims):
    (lh, ll), (rh, rl) = left, right
    dot = lambda a, b: lax.dot_general(a, b, (dims, ((), ())), preferred_element_type=F32)
    return dot(lh, rh) + (dot(lh, rl) + dot(ll, rh))


def call(kernel, shapes, scalars, arrays, scratch=()):
    return pl.pallas_call(
        kernel,
        in_specs=[SMEM] * len(scalars) + [VMEM] * len(arrays),
        out_specs=[VMEM] * len(shapes),
        out_shape=[jax.ShapeDtypeStruct(s, F32) for s in shapes],
        scratch_shapes=[pltpu.VMEM(s, F32) for s in scratch],
        compiler_params=pltpu.CompilerParams(vmem_limit_bytes=LIMIT),
    )(*scalars, *arrays)


def place_fitted(total, out):
    width = out.shape[2]
    for o in range(2):
        out[o] = total[:, o * width : (o + 1) * width]


def fit_kernel(order, metric, *refs):
    blocks, out = refs[:-1], refs[-1]
    depth = metric.shape[0]
    total = jnp.zeros((depth, blocks[0].shape[1]), F32)
    for k, block in enumerate(blocks):
        place = pl.multiple_of(order[k] * depth, depth)
        total += dot3(split(metric[:, pl.ds(place, depth)]), split(block[...]), PLAIN)
    place_fitted(total, out)


def fit_whole_kernel(metric, every, out):
    depth = metric.shape[0]
    total = jnp.zeros((depth, every.shape[1]), F32)
    for k in range(metric.shape[1] // depth):
        block = slice(k * depth, (k + 1) * depth)
        total += dot3(split(metric[:, block]), split(every[block]), PLAIN)
    place_fitted(total, out)


def select_kernel(table, *refs):
    blocks, outs = refs[:4], refs[4:]
    for d in range(4):
        for s in range(4):
            outs[d][s] = jnp.where(table[d, s] == 1, blocks[s][1], blocks[s][0])


def fold_kernel(table, *refs):
    arrived, outs = refs[:4], refs[4:]
    for s in range(4):
        for o in range(2):
            total = jnp.where(table[0, s] == o, arrived[0][s], 0.0)
            for e in range(1, 4):
                total += jnp.where(table[e, s] == o, arrived[e][s], 0.0)
            outs[s][o] = total


def assemble(half, arrived):
    for d in range(4):
        half[4 * d : 4 * d + 4] = arrived[d][...]


def corner_couplings(slots, half, mine, other):
    for k in range(16):
        out = mine if k < 8 else other
        out[k % 8, 0] = dot3(split(half[slots[0, k]]), split(half[slots[1, k]]), ROWS)


def corner_kernel(slots, half, mine, other):
    corner_couplings(slots, half, mine, other)


def assembled_corner_kernel(slots, *refs):
    half, mine, other = refs[4:]
    assemble(half, refs[:4])
    corner_couplings(slots, half, mine, other)


def mixed_couplings(slots, half0, half1, out, start):
    for k in range(8):
        first, second = slots[0, start + k], slots[1, start + k]
        out[k, 0] = dot3(split(half0[first]), split(half1[second]), ROWS)
        out[k, 1] = dot3(split(half1[first]), split(half0[second]), ROWS)


def mixed_kernel(slots, half0, half1, out):
    mixed_couplings(slots, half0, half1, out, 0)


def assembled_mixed_kernel(slots, half0, *refs):
    half1, out = refs[4:]
    assemble(half1, refs[:4])
    mixed_couplings(slots, half0, half1, out, 8)


PLACES = [(0, 0), (0, 1), (1, 0), (1, 1), (2, 0), (2, 1), (1, 2), (1, 3)]


def gradient_sum(total, forward_at, back_at, slots, half, parts):
    for k in range(16):
        array, at = PLACES[k % 8]
        part = parts[array + (0 if k < 8 else 3)]
        first, second = slots[0, k], slots[1, k]
        forward = split(part[at, forward_at])
        back = forward if forward_at == back_at else split(part[at, back_at])
        total[first] += dot3(split(half[second]), forward, COLS)
        total[second] += dot3(split(half[first]), back, PLAIN)


def begin_kernel(forward_at, back_at, slots, half, *refs):
    out = refs[-1]
    out[...] = jnp.zeros_like(out)
    gradient_sum(out, forward_at, back_at, slots, half, refs[:6])


def finish_kernel(forward_at, back_at, slots, half, *refs):
    outs, total = refs[7:-1], refs[-1]
    total[...] = refs[6][...]
    gradient_sum(total, forward_at, back_at, slots, half, refs[:6])
    for d in range(4):
        outs[d][...] = total[4 * d : 4 * d + 4]


def body(integrals, metric, occ_energy, vir_energy, pair_orbitals):
    rows, occ_count, vir_count = integrals.shape
    width = vir_count // 2
    orb_count = lax.axis_size("orb")
    my_index = lax.axis_index("orb")
    my_x, my_z = my_index // 4, my_index % 4
    pair_count = pair_orbitals.shape[0] // orb_count
    pair_ends = pair_orbitals.reshape(orb_count, 2 * pair_count)
    owners = jnp.arange(orb_count, dtype=jnp.int32)[None, :, None]
    picks = jnp.max(
        jnp.where(pair_ends[:, None] // occ_count == owners, pair_ends[:, None] % occ_count, -1), 2
    )
    my_pairs = lax.dynamic_slice_in_dim(pair_orbitals, my_index * pair_count, pair_count, 0)

    def at(table, index, axis):
        hot = index.reshape((-1, 1)) == jnp.arange(table.shape[axis], dtype=jnp.int32)
        hot = hot.reshape((-1,) + (1,) * axis + (table.shape[axis],) + (1,) * (table.ndim - 1 - axis))
        return jnp.moveaxis(jnp.sum(jnp.where(hot, table[None], 0), axis=axis + 1), 0, axis)

    my_aux = lax.axis_index("aux")
    my_y, my_core = my_aux // 2, my_aux % 2
    ring = jnp.arange(4, dtype=jnp.int32)
    away = (jnp.arange(2, dtype=jnp.int32)[:, None] + my_core) % 2
    order = (away * 4 + (ring[None, :] + my_y) % 4)[:, :, None] * 2 + jnp.arange(2)[None, None, :]
    hot = order.reshape(-1)[:, None] == jnp.arange(pair_count, dtype=jnp.int32)[None, :]
    near_pairs = jnp.sum(jnp.where(hot[:, :, None], my_pairs[None], 0), axis=1)
    blocks = near_pairs // occ_count
    away_x, away_z = (blocks // 4 - my_x) % 4, (blocks % 4 - my_z) % 4
    slots = jnp.where(my_core == 0, away_z * 4 + away_x, away_x * 4 + away_z).T
    same_z = (my_x + ring) % 4 * 4 + my_z
    same_x = my_x * 4 + (my_z + ring) % 4
    near = jnp.where(my_core == 0, same_z, same_x)
    table = at(at(picks, jnp.where(my_core == 0, same_x, same_z), 0), near, 1)
    occ_hot = near_pairs[:2, :, None] == jnp.arange(occ_energy.shape[0], dtype=jnp.int32)
    shift = jnp.sum(jnp.where(occ_hot, occ_energy, 0.0), axis=(1, 2))

    def up(x):
        return lax.ppermute(x, "aux", [(k, (k + 2) % 8) for k in range(8)])

    def down(x):
        return lax.ppermute(x, "aux", [(k, (k + 6) % 8) for k in range(8)])

    def across(x):
        return lax.ppermute(x, "aux", [(k, k ^ 1) for k in range(8)])

    def move(step, by_x):
        perm = []
        for a in range(8):
            for x in range(4):
                for z in range(4):
                    if a % 2 == by_x:
                        to = (x + step) % 4 * 4 + z
                    else:
                        to = x * 4 + (z + step) % 4
                    perm.append((a * 16 + x * 4 + z, a * 16 + to))
        return lambda v: lax.ppermute(v, ("aux", "orb"), perm)

    near_moves = move(1, 0), move(3, 0), move(2, 0)
    far_moves = move(1, 1), move(3, 1), move(2, 1)

    def part_of(h):
        return integrals[:, :, h * width : (h + 1) * width].reshape(rows, occ_count * width)

    cores = jnp.arange(2, dtype=jnp.int32)[None, :]
    metric_order = (((my_y + ring)[:, None] % 4) * 2 + (my_core + cores) % 2).reshape(-1)
    strip = (2, rows, width)
    piece = (4, rows, width)

    def exchange(parts, moves):
        forth, back, across_ring = moves
        return [parts[0], back(parts[3]), across_ring(parts[2]), forth(parts[1])]

    def select(arrived):
        return call(select_kernel, [piece] * 4, [table], arrived)

    def fold(arrived):
        sums = exchange(call(fold_kernel, [strip] * 4, [table], arrived), near_moves)
        return sum(sums[1:], sums[0])

    def reduce_start(mine, other):
        theirs = across(other)
        a2, b2 = up(mine[4:5] + theirs[4:5]), down(mine[5:6] + theirs[5:6])
        return mine, theirs, a2, b2

    def reduce_end(state):
        mine, theirs, a2, b2 = state
        upward = jnp.concatenate([mine[2:3] + theirs[2:3] + a2, mine[3:4] + theirs[3:4]], 0)
        downward = jnp.concatenate([mine[6:7] + theirs[6:7], mine[7:8] + theirs[7:8] + b2], 0)
        return mine[0:2] + theirs[0:2] + up(upward) + down(downward)

    def amplitude(total, starts):
        parts = []
        for k, (i, j) in enumerate(starts):
            column = vir_energy[i : i + width][None, :, None]
            row = vir_energy[j : j + width][None, None, :]
            parts.append(-total[:, k] / (column + row - shift[:, None, None]))
        return jnp.stack(parts, axis=1)

    def spread_start(own):
        return own, up(own), down(own)

    def spread_far(state):
        own, below, above = state
        far = jnp.concatenate([up(below[0:1]), down(above[1:2])], 0)
        return [own, jnp.concatenate([above, below], 0), far]

    def spread_end(ours):
        return list(ours) + [across(x) for x in ours]

    def begin(forward_at, back_at, half, amplitudes, slots):
        kernel = functools.partial(begin_kernel, forward_at, back_at)
        return call(kernel, [whole], [slots], [half, *amplitudes])[0]

    def finish(forward_at, back_at, half, amplitudes, start):
        kernel = functools.partial(finish_kernel, forward_at, back_at)
        return call(kernel, [piece] * 4, [slots], [half, *amplitudes, start], [whole])

    eight = (8, 1, width, width)
    sixteen = (8, 2, width, width)
    whole = (orb_count, rows, width)
    own = part_of(0)
    below, above = up(own), down(own)
    far = jnp.concatenate([up(below[: rows // 2]), down(above[rows // 2 :])], axis=0)
    blocks = [b for x in (own, above, far, below) for b in (x, across(x))]
    later, far = together((part_of(1), far))
    every = lax.all_gather(later, "aux", axis=0, tiled=True)
    (fitted,) = call(fit_kernel, [strip], [metric_order], [metric, *blocks])
    chosen, every = together((select(exchange([fitted] * 4, near_moves)), every))
    arrived = exchange(chosen, far_moves)
    (fitted,) = call(fit_whole_kernel, [strip], [], [metric, every])
    fitted, arrived = together((fitted, arrived))
    half0, mine, other = call(assembled_corner_kernel, [whole, eight, eight], [slots], arrived)
    near = exchange([fitted] * 4, near_moves)
    state, near = together((reduce_start(mine, other), near))
    arrived = exchange(select(near), far_moves)
    spread = spread_start(amplitude(reduce_end(state), [(0, 0)]))
    arrived, spread = together((arrived, spread))
    corner = spread_far(spread)
    half1, other = call(assembled_mixed_kernel, [whole, sixteen], [slots], [half0, *arrived])
    (mine,) = call(mixed_kernel, [sixteen], [slots], [half0, half1])
    state = reduce_start(mine, other)
    state, corner, late_half1 = together((state, corner, half1))
    mine, other = call(corner_kernel, [eight, eight], [slots], [late_half1])
    total = reduce_end(state)
    spread = spread_start(amplitude(total, [(0, width), (width, 0)]))
    grad0 = begin(0, 0, half0, spread_end(corner), slots)
    spread, grad0, mine, other = together((spread, grad0, mine, other))
    mixed = spread_far(spread)
    mine, mixed[2] = together((mine, mixed[2]))
    mixed = spread_end(mixed)
    grad0 = finish(0, 1, half1, mixed, grad0)
    state = reduce_start(mine, other)
    later_slots, state, grad0 = together((slots, state, grad0))
    grad1 = begin(1, 0, half0, mixed, later_slots)
    back = exchange(grad0, far_moves)
    spread = spread_start(amplitude(reduce_end(state), [(width, width)]))
    spread, grad1, back = together((spread, grad1, back))
    last = spread_end(spread_far(spread))
    first, last = together((fold(back), last))
    second = fold(exchange(finish(0, 0, half1, last, grad1), far_moves))
    return jnp.concatenate([first, second], axis=2).transpose(1, 0, 2)


def solution(mesh):
    return jax.shard_map(
        body,
        mesh=mesh,
        in_specs=(P("aux", "orb", None), P("aux", None), P(), P(), P()),
        out_specs=P("aux", "orb", None),
        check_vma=False,
    )
```

```python
import functools

import jax
import jax.numpy as jnp
from jax import lax
from jax.experimental import pallas as pl
from jax.experimental.pallas import tpu as pltpu
from jax.sharding import PartitionSpec as P

F32 = jnp.float32
LIMIT = 16 * 1024 * 1024
ROWS = ((0,), (0,))
COLS = ((1,), (1,))
PLAIN = ((1,), (0,))
VMEM = pl.BlockSpec(memory_space=pltpu.VMEM)
SMEM = pl.BlockSpec(memory_space=pltpu.SMEM)
together = lax.optimization_barrier


def split(x):
    high = x.astype(jnp.bfloat16)
    return high, (x - high.astype(F32)).astype(jnp.bfloat16)


def dot3(left, right, dims):
    (lh, ll), (rh, rl) = left, right
    dot = lambda a, b: lax.dot_general(a, b, (dims, ((), ())), preferred_element_type=F32)
    return dot(lh, rh) + (dot(lh, rl) + dot(ll, rh))


def call(kernel, shapes, scalars, arrays, scratch=()):
    return pl.pallas_call(
        kernel,
        in_specs=[SMEM] * len(scalars) + [VMEM] * len(arrays),
        out_specs=[VMEM] * len(shapes),
        out_shape=[jax.ShapeDtypeStruct(s, F32) for s in shapes],
        scratch_shapes=[pltpu.VMEM(s, F32) for s in scratch],
        compiler_params=pltpu.CompilerParams(vmem_limit_bytes=LIMIT),
    )(*scalars, *arrays)


def place_fitted(total, out):
    width = out.shape[2]
    for o in range(2):
        out[o] = total[:, o * width : (o + 1) * width]


def fit_kernel(order, metric, *refs):
    blocks, out = refs[:-1], refs[-1]
    depth = metric.shape[0]
    total = jnp.zeros((depth, blocks[0].shape[1]), F32)
    for k, block in enumerate(blocks):
        place = pl.multiple_of(order[k] * depth, depth)
        total += dot3(split(metric[:, pl.ds(place, depth)]), split(block[...]), PLAIN)
    place_fitted(total, out)


def select_kernel(table, *refs):
    blocks, outs = refs[:4], refs[4:]
    for d in range(4):
        for s in range(4):
            outs[d][s] = jnp.where(table[d, s] == 1, blocks[s][1], blocks[s][0])


def fold_kernel(table, *refs):
    arrived, outs = refs[:4], refs[4:]
    for s in range(4):
        for o in range(2):
            total = jnp.where(table[0, s] == o, arrived[0][s], 0.0)
            for e in range(1, 4):
                total += jnp.where(table[e, s] == o, arrived[e][s], 0.0)
            outs[s][o] = total


def assemble(half, arrived):
    for d in range(4):
        half[4 * d : 4 * d + 4] = arrived[d][...]


def corner_couplings(slots, half, mine, other):
    for k in range(16):
        out = mine if k < 8 else other
        out[k % 8, 0] = dot3(split(half[slots[0, k]]), split(half[slots[1, k]]), ROWS)


def corner_kernel(slots, half, mine, other):
    corner_couplings(slots, half, mine, other)


def assembled_corner_kernel(slots, *refs):
    half, mine, other = refs[4:]
    assemble(half, refs[:4])
    corner_couplings(slots, half, mine, other)


def mixed_couplings(slots, half0, half1, out, start):
    for k in range(8):
        first, second = slots[0, start + k], slots[1, start + k]
        out[k, 0] = dot3(split(half0[first]), split(half1[second]), ROWS)
        out[k, 1] = dot3(split(half1[first]), split(half0[second]), ROWS)


def mixed_kernel(slots, half0, half1, out):
    mixed_couplings(slots, half0, half1, out, 0)


def assembled_mixed_kernel(slots, half0, *refs):
    half1, out = refs[4:]
    assemble(half1, refs[:4])
    mixed_couplings(slots, half0, half1, out, 8)


PLACES = [(0, 0), (0, 1), (1, 0), (1, 1), (2, 0), (2, 1), (1, 2), (1, 3)]


def gradient_sum(total, forward_at, back_at, slots, half, parts):
    for k in range(16):
        array, at = PLACES[k % 8]
        part = parts[array + (0 if k < 8 else 3)]
        first, second = slots[0, k], slots[1, k]
        forward = split(part[at, forward_at])
        back = forward if forward_at == back_at else split(part[at, back_at])
        total[first] += dot3(split(half[second]), forward, COLS)
        total[second] += dot3(split(half[first]), back, PLAIN)


def begin_kernel(forward_at, back_at, slots, half, *refs):
    out = refs[-1]
    out[...] = jnp.zeros_like(out)
    gradient_sum(out, forward_at, back_at, slots, half, refs[:6])


def finish_kernel(forward_at, back_at, slots, half, *refs):
    outs, total = refs[7:-1], refs[-1]
    total[...] = refs[6][...]
    gradient_sum(total, forward_at, back_at, slots, half, refs[:6])
    for d in range(4):
        outs[d][...] = total[4 * d : 4 * d + 4]


def body(integrals, metric, occ_energy, vir_energy, pair_orbitals):
    rows, occ_count, vir_count = integrals.shape
    width = vir_count // 2
    orb_count = lax.axis_size("orb")
    my_index = lax.axis_index("orb")
    my_x, my_z = my_index // 4, my_index % 4
    pair_count = pair_orbitals.shape[0] // orb_count
    pair_ends = pair_orbitals.reshape(orb_count, 2 * pair_count)
    owners = jnp.arange(orb_count, dtype=jnp.int32)[None, :, None]
    picks = jnp.max(
        jnp.where(pair_ends[:, None] // occ_count == owners, pair_ends[:, None] % occ_count, -1), 2
    )
    my_pairs = lax.dynamic_slice_in_dim(pair_orbitals, my_index * pair_count, pair_count, 0)

    def at(table, index, axis):
        hot = index.reshape((-1, 1)) == jnp.arange(table.shape[axis], dtype=jnp.int32)
        hot = hot.reshape((-1,) + (1,) * axis + (table.shape[axis],) + (1,) * (table.ndim - 1 - axis))
        return jnp.moveaxis(jnp.sum(jnp.where(hot, table[None], 0), axis=axis + 1), 0, axis)

    my_aux = lax.axis_index("aux")
    my_y, my_core = my_aux // 2, my_aux % 2
    ring = jnp.arange(4, dtype=jnp.int32)
    away = (jnp.arange(2, dtype=jnp.int32)[:, None] + my_core) % 2
    order = (away * 4 + (ring[None, :] + my_y) % 4)[:, :, None] * 2 + jnp.arange(2)[None, None, :]
    hot = order.reshape(-1)[:, None] == jnp.arange(pair_count, dtype=jnp.int32)[None, :]
    near_pairs = jnp.sum(jnp.where(hot[:, :, None], my_pairs[None], 0), axis=1)
    blocks = near_pairs // occ_count
    away_x, away_z = (blocks // 4 - my_x) % 4, (blocks % 4 - my_z) % 4
    slots = jnp.where(my_core == 0, away_z * 4 + away_x, away_x * 4 + away_z).T
    same_z = (my_x + ring) % 4 * 4 + my_z
    same_x = my_x * 4 + (my_z + ring) % 4
    near = jnp.where(my_core == 0, same_z, same_x)
    table = at(at(picks, jnp.where(my_core == 0, same_x, same_z), 0), near, 1)
    occ_hot = near_pairs[:2, :, None] == jnp.arange(occ_energy.shape[0], dtype=jnp.int32)
    shift = jnp.sum(jnp.where(occ_hot, occ_energy, 0.0), axis=(1, 2))

    def up(x):
        return lax.ppermute(x, "aux", [(k, (k + 2) % 8) for k in range(8)])

    def down(x):
        return lax.ppermute(x, "aux", [(k, (k + 6) % 8) for k in range(8)])

    def across(x):
        return lax.ppermute(x, "aux", [(k, k ^ 1) for k in range(8)])

    def move(step, by_x):
        perm = []
        for a in range(8):
            for x in range(4):
                for z in range(4):
                    if a % 2 == by_x:
                        to = (x + step) % 4 * 4 + z
                    else:
                        to = x * 4 + (z + step) % 4
                    perm.append((a * 16 + x * 4 + z, a * 16 + to))
        return lambda v: lax.ppermute(v, ("aux", "orb"), perm)

    near_moves = move(1, 0), move(3, 0), move(2, 0)
    far_moves = move(1, 1), move(3, 1), move(2, 1)

    def part_of(h):
        return integrals[:, :, h * width : (h + 1) * width].reshape(rows, occ_count * width)

    cores = jnp.arange(2, dtype=jnp.int32)[None, :]
    metric_order = (((my_y + ring)[:, None] % 4) * 2 + (my_core + cores) % 2).reshape(-1)
    strip = (2, rows, width)
    piece = (4, rows, width)

    def exchange(parts, moves):
        forth, back, across_ring = moves
        return [parts[0], back(parts[3]), across_ring(parts[2]), forth(parts[1])]

    def select(arrived):
        return call(select_kernel, [piece] * 4, [table], arrived)

    def fold(arrived):
        sums = exchange(call(fold_kernel, [strip] * 4, [table], arrived), near_moves)
        return sum(sums[1:], sums[0])

    def reduce_start(mine, other):
        theirs = across(other)
        a2, b2 = up(mine[4:5] + theirs[4:5]), down(mine[5:6] + theirs[5:6])
        return mine, theirs, a2, b2

    def reduce_end(state):
        mine, theirs, a2, b2 = state
        upward = jnp.concatenate([mine[2:3] + theirs[2:3] + a2, mine[3:4] + theirs[3:4]], 0)
        downward = jnp.concatenate([mine[6:7] + theirs[6:7], mine[7:8] + theirs[7:8] + b2], 0)
        return mine[0:2] + theirs[0:2] + up(upward) + down(downward)

    def amplitude(total, starts):
        parts = []
        for k, (i, j) in enumerate(starts):
            column = vir_energy[i : i + width][None, :, None]
            row = vir_energy[j : j + width][None, None, :]
            parts.append(-total[:, k] / (column + row - shift[:, None, None]))
        return jnp.stack(parts, axis=1)

    def spread_start(own):
        return own, up(own), down(own)

    def spread_far(state):
        own, below, above = state
        far = jnp.concatenate([up(below[0:1]), down(above[1:2])], 0)
        return [own, jnp.concatenate([above, below], 0), far]

    def spread_end(ours):
        return list(ours) + [across(x) for x in ours]

    def begin(forward_at, back_at, half, amplitudes, slots):
        kernel = functools.partial(begin_kernel, forward_at, back_at)
        return call(kernel, [whole], [slots], [half, *amplitudes])[0]

    def finish(forward_at, back_at, half, amplitudes, start):
        kernel = functools.partial(finish_kernel, forward_at, back_at)
        return call(kernel, [piece] * 4, [slots], [half, *amplitudes, start], [whole])

    eight = (8, 1, width, width)
    sixteen = (8, 2, width, width)
    whole = (orb_count, rows, width)
    def gather(own):
        below, above = up(own), down(own)
        far = jnp.concatenate([up(below[: rows // 2]), down(above[rows // 2 :])], axis=0)
        return [b for x in (own, above, far, below) for b in (x, across(x))]

    blocks = gather(part_of(0))
    (fitted,) = call(fit_kernel, [strip], [metric_order], [metric, *blocks])
    fitted, later = together((fitted, part_of(1)))
    arrived = exchange(select(exchange([fitted] * 4, near_moves)), far_moves)
    (fitted,) = call(fit_kernel, [strip], [metric_order], [metric, *gather(later)])
    fitted, arrived = together((fitted, arrived))
    half0, mine, other = call(assembled_corner_kernel, [whole, eight, eight], [slots], arrived)
    near = exchange([fitted] * 4, near_moves)
    state, near = together((reduce_start(mine, other), near))
    arrived = exchange(select(near), far_moves)
    spread = spread_start(amplitude(reduce_end(state), [(0, 0)]))
    corner = spread_far(spread)
    half1, other = call(assembled_mixed_kernel, [whole, sixteen], [slots], [half0, *arrived])
    half1, corner = together((half1, corner))
    (mine,) = call(mixed_kernel, [sixteen], [slots], [half0, half1])
    state = reduce_start(mine, other)
    state, corner, late_half1 = together((state, corner, half1))
    mine, other = call(corner_kernel, [eight, eight], [slots], [late_half1])
    total = reduce_end(state)
    spread = spread_start(amplitude(total, [(0, width), (width, 0)]))
    grad0 = begin(0, 0, half0, spread_end(corner), slots)
    spread, grad0, mine, other = together((spread, grad0, mine, other))
    mixed = spread_far(spread)
    mine, mixed[2] = together((mine, mixed[2]))
    mixed = spread_end(mixed)
    grad0 = finish(0, 1, half1, mixed, grad0)
    state = reduce_start(mine, other)
    later_slots, state, grad0 = together((slots, state, grad0))
    grad1 = begin(1, 0, half0, mixed, later_slots)
    back = exchange(grad0, far_moves)
    spread = spread_start(amplitude(reduce_end(state), [(width, width)]))
    spread, grad1, back = together((spread, grad1, back))
    last = spread_end(spread_far(spread))
    first, last = together((fold(back), last))
    second = fold(exchange(finish(0, 0, half1, last, grad1), far_moves))
    return jnp.concatenate([first, second], axis=2).transpose(1, 0, 2)


def solution(mesh):
    return jax.shard_map(
        body,
        mesh=mesh,
        in_specs=(P("aux", "orb", None), P("aux", None), P(), P(), P()),
        out_specs=P("aux", "orb", None),
        check_vma=False,
    )
```

```python
import functools

import jax
import jax.numpy as jnp
from jax import lax
from jax.experimental import pallas as pl
from jax.experimental.pallas import tpu as pltpu
from jax.sharding import PartitionSpec as P

F32 = jnp.float32
LIMIT = 16 * 1024 * 1024
ROWS = ((0,), (0,))
COLS = ((1,), (1,))
PLAIN = ((1,), (0,))
VMEM = pl.BlockSpec(memory_space=pltpu.VMEM)
SMEM = pl.BlockSpec(memory_space=pltpu.SMEM)
together = lax.optimization_barrier


def split(x):
    high = x.astype(jnp.bfloat16)
    return high, (x - high.astype(F32)).astype(jnp.bfloat16)


def dot3(left, right, dims):
    (lh, ll), (rh, rl) = left, right
    dot = lambda a, b: lax.dot_general(a, b, (dims, ((), ())), preferred_element_type=F32)
    return dot(lh, rh) + (dot(lh, rl) + dot(ll, rh))


def call(kernel, shapes, scalars, arrays, scratch=()):
    return pl.pallas_call(
        kernel,
        in_specs=[SMEM] * len(scalars) + [VMEM] * len(arrays),
        out_specs=[VMEM] * len(shapes),
        out_shape=[jax.ShapeDtypeStruct(s, F32) for s in shapes],
        scratch_shapes=[pltpu.VMEM(s, F32) for s in scratch],
        compiler_params=pltpu.CompilerParams(vmem_limit_bytes=LIMIT),
    )(*scalars, *arrays)


def place_fitted(total, out):
    width = out.shape[2]
    for o in range(2):
        out[o] = total[:, o * width : (o + 1) * width]


def fit_kernel(order, metric, *refs):
    blocks, out = refs[:-1], refs[-1]
    depth = metric.shape[0]
    total = jnp.zeros((depth, blocks[0].shape[1]), F32)
    for k, block in enumerate(blocks):
        place = pl.multiple_of(order[k] * depth, depth)
        total += dot3(split(metric[:, pl.ds(place, depth)]), split(block[...]), PLAIN)
    place_fitted(total, out)


def select_kernel(table, *refs):
    blocks, outs = refs[:4], refs[4:]
    for d in range(4):
        for s in range(4):
            outs[d][s] = jnp.where(table[d, s] == 1, blocks[s][1], blocks[s][0])


def fold_kernel(table, *refs):
    arrived, outs = refs[:4], refs[4:]
    for s in range(4):
        for o in range(2):
            total = jnp.where(table[0, s] == o, arrived[0][s], 0.0)
            for e in range(1, 4):
                total += jnp.where(table[e, s] == o, arrived[e][s], 0.0)
            outs[s][o] = total


def assemble(half, arrived):
    for d in range(4):
        half[4 * d : 4 * d + 4] = arrived[d][...]


def corner_couplings(slots, half, mine, other):
    for k in range(16):
        out = mine if k < 8 else other
        out[k % 8, 0] = dot3(split(half[slots[0, k]]), split(half[slots[1, k]]), ROWS)


def corner_kernel(slots, half, mine, other):
    corner_couplings(slots, half, mine, other)


def assembled_corner_kernel(slots, *refs):
    half, mine, other = refs[4:]
    assemble(half, refs[:4])
    corner_couplings(slots, half, mine, other)


def mixed_couplings(slots, half0, half1, out, start):
    for k in range(8):
        first, second = slots[0, start + k], slots[1, start + k]
        out[k, 0] = dot3(split(half0[first]), split(half1[second]), ROWS)
        out[k, 1] = dot3(split(half1[first]), split(half0[second]), ROWS)


def mixed_kernel(slots, half0, half1, out):
    mixed_couplings(slots, half0, half1, out, 0)


def assembled_mixed_kernel(slots, half0, *refs):
    half1, out = refs[4:]
    assemble(half1, refs[:4])
    mixed_couplings(slots, half0, half1, out, 8)


PLACES = [(0, 0), (0, 1), (1, 0), (1, 1), (2, 0), (2, 1), (1, 2), (1, 3)]


def gradient_sum(total, forward_at, back_at, slots, half, parts):
    for k in range(16):
        array, at = PLACES[k % 8]
        part = parts[array + (0 if k < 8 else 3)]
        first, second = slots[0, k], slots[1, k]
        forward = split(part[at, forward_at])
        back = forward if forward_at == back_at else split(part[at, back_at])
        total[first] += dot3(split(half[second]), forward, COLS)
        total[second] += dot3(split(half[first]), back, PLAIN)


def begin_kernel(forward_at, back_at, slots, half, *refs):
    out = refs[-1]
    out[...] = jnp.zeros_like(out)
    gradient_sum(out, forward_at, back_at, slots, half, refs[:6])


def finish_kernel(forward_at, back_at, slots, half, *refs):
    outs, total = refs[7:-1], refs[-1]
    total[...] = refs[6][...]
    gradient_sum(total, forward_at, back_at, slots, half, refs[:6])
    for d in range(4):
        outs[d][...] = total[4 * d : 4 * d + 4]


def body(integrals, metric, occ_energy, vir_energy, pair_orbitals):
    rows, occ_count, vir_count = integrals.shape
    width = vir_count // 2
    orb_count = lax.axis_size("orb")
    my_index = lax.axis_index("orb")
    my_x, my_z = my_index // 4, my_index % 4
    pair_count = pair_orbitals.shape[0] // orb_count
    pair_ends = pair_orbitals.reshape(orb_count, 2 * pair_count)
    owners = jnp.arange(orb_count, dtype=jnp.int32)[None, :, None]
    picks = jnp.max(
        jnp.where(pair_ends[:, None] // occ_count == owners, pair_ends[:, None] % occ_count, -1), 2
    )
    my_pairs = lax.dynamic_slice_in_dim(pair_orbitals, my_index * pair_count, pair_count, 0)

    def at(table, index, axis):
        hot = index.reshape((-1, 1)) == jnp.arange(table.shape[axis], dtype=jnp.int32)
        hot = hot.reshape((-1,) + (1,) * axis + (table.shape[axis],) + (1,) * (table.ndim - 1 - axis))
        return jnp.moveaxis(jnp.sum(jnp.where(hot, table[None], 0), axis=axis + 1), 0, axis)

    my_aux = lax.axis_index("aux")
    my_y, my_core = my_aux // 2, my_aux % 2
    ring = jnp.arange(4, dtype=jnp.int32)
    away = (jnp.arange(2, dtype=jnp.int32)[:, None] + my_core) % 2
    order = (away * 4 + (ring[None, :] + my_y) % 4)[:, :, None] * 2 + jnp.arange(2)[None, None, :]
    hot = order.reshape(-1)[:, None] == jnp.arange(pair_count, dtype=jnp.int32)[None, :]
    near_pairs = jnp.sum(jnp.where(hot[:, :, None], my_pairs[None], 0), axis=1)
    blocks = near_pairs // occ_count
    away_x, away_z = (blocks // 4 - my_x) % 4, (blocks % 4 - my_z) % 4
    slots = jnp.where(my_core == 0, away_z * 4 + away_x, away_x * 4 + away_z).T
    same_z = (my_x + ring) % 4 * 4 + my_z
    same_x = my_x * 4 + (my_z + ring) % 4
    near = jnp.where(my_core == 0, same_z, same_x)
    table = at(at(picks, jnp.where(my_core == 0, same_x, same_z), 0), near, 1)
    occ_hot = near_pairs[:2, :, None] == jnp.arange(occ_energy.shape[0], dtype=jnp.int32)
    shift = jnp.sum(jnp.where(occ_hot, occ_energy, 0.0), axis=(1, 2))

    def up(x):
        return lax.ppermute(x, "aux", [(k, (k + 2) % 8) for k in range(8)])

    def down(x):
        return lax.ppermute(x, "aux", [(k, (k + 6) % 8) for k in range(8)])

    def across(x):
        return lax.ppermute(x, "aux", [(k, k ^ 1) for k in range(8)])

    def move(step, by_x):
        perm = []
        for a in range(8):
            for x in range(4):
                for z in range(4):
                    if a % 2 == by_x:
                        to = (x + step) % 4 * 4 + z
                    else:
                        to = x * 4 + (z + step) % 4
                    perm.append((a * 16 + x * 4 + z, a * 16 + to))
        return lambda v: lax.ppermute(v, ("aux", "orb"), perm)

    near_moves = move(1, 0), move(3, 0), move(2, 0)
    far_moves = move(1, 1), move(3, 1), move(2, 1)

    def part_of(h):
        return integrals[:, :, h * width : (h + 1) * width].reshape(rows, occ_count * width)

    cores = jnp.arange(2, dtype=jnp.int32)[None, :]
    metric_order = (((my_y + ring)[:, None] % 4) * 2 + (my_core + cores) % 2).reshape(-1)
    strip = (2, rows, width)
    piece = (4, rows, width)

    def exchange(parts, moves):
        forth, back, across_ring = moves
        return [parts[0], back(parts[3]), across_ring(parts[2]), forth(parts[1])]

    def select(arrived):
        return call(select_kernel, [piece] * 4, [table], arrived)

    def fold(arrived):
        sums = exchange(call(fold_kernel, [strip] * 4, [table], arrived), near_moves)
        return sum(sums[1:], sums[0])

    def reduce_start(mine, other):
        theirs = across(other)
        a2, b2 = up(mine[4:5] + theirs[4:5]), down(mine[5:6] + theirs[5:6])
        return mine, theirs, a2, b2

    def reduce_end(state):
        mine, theirs, a2, b2 = state
        upward = jnp.concatenate([mine[2:3] + theirs[2:3] + a2, mine[3:4] + theirs[3:4]], 0)
        downward = jnp.concatenate([mine[6:7] + theirs[6:7], mine[7:8] + theirs[7:8] + b2], 0)
        return mine[0:2] + theirs[0:2] + up(upward) + down(downward)

    def amplitude(total, starts):
        parts = []
        for k, (i, j) in enumerate(starts):
            column = vir_energy[i : i + width][None, :, None]
            row = vir_energy[j : j + width][None, None, :]
            parts.append(-total[:, k] / (column + row - shift[:, None, None]))
        return jnp.stack(parts, axis=1)

    def spread_start(own):
        return own, up(own), down(own)

    def spread_far(state):
        own, below, above = state
        far = jnp.concatenate([up(below[0:1]), down(above[1:2])], 0)
        return [own, jnp.concatenate([above, below], 0), far]

    def spread_end(ours):
        return list(ours) + [across(x) for x in ours]

    def begin(forward_at, back_at, half, amplitudes, slots):
        kernel = functools.partial(begin_kernel, forward_at, back_at)
        return call(kernel, [whole], [slots], [half, *amplitudes])[0]

    def finish(forward_at, back_at, half, amplitudes, start):
        kernel = functools.partial(finish_kernel, forward_at, back_at)
        return call(kernel, [piece] * 4, [slots], [half, *amplitudes, start], [whole])

    eight = (8, 1, width, width)
    sixteen = (8, 2, width, width)
    whole = (orb_count, rows, width)
    def gather(own):
        below, above = up(own), down(own)
        far = jnp.concatenate([up(below[: rows // 2]), down(above[rows // 2 :])], axis=0)
        return [b for x in (own, above, far, below) for b in (x, across(x))]

    blocks, later = together((gather(part_of(0)), part_of(1)))
    (fitted,) = call(fit_kernel, [strip], [metric_order], [metric, *blocks])
    arrived = exchange(select(exchange([fitted] * 4, near_moves)), far_moves)
    (fitted,) = call(fit_kernel, [strip], [metric_order], [metric, *gather(later)])
    fitted, arrived = together((fitted, arrived))
    half0, mine, other = call(assembled_corner_kernel, [whole, eight, eight], [slots], arrived)
    near = exchange([fitted] * 4, near_moves)
    state, near = together((reduce_start(mine, other), near))
    arrived = exchange(select(near), far_moves)
    spread = spread_start(amplitude(reduce_end(state), [(0, 0)]))
    corner = spread_far(spread)
    arrived, corner[1] = together((arrived, corner[1]))
    half1, other = call(assembled_mixed_kernel, [whole, sixteen], [slots], [half0, *arrived])
    half1, corner[2] = together((half1, corner[2]))
    (mine,) = call(mixed_kernel, [sixteen], [slots], [half0, half1])
    state = reduce_start(mine, other)
    state, corner, late_half1 = together((state, corner, half1))
    mine, other = call(corner_kernel, [eight, eight], [slots], [late_half1])
    total = reduce_end(state)
    spread = spread_start(amplitude(total, [(0, width), (width, 0)]))
    grad0 = begin(0, 0, half0, spread_end(corner), slots)
    spread, grad0, mine, other = together((spread, grad0, mine, other))
    mixed = spread_far(spread)
    mine, mixed[2] = together((mine, mixed[2]))
    mixed = spread_end(mixed)
    grad0 = finish(0, 1, half1, mixed, grad0)
    state = reduce_start(mine, other)
    later_slots, state, grad0 = together((slots, state, grad0))
    grad1 = begin(1, 0, half0, mixed, later_slots)
    back = exchange(grad0, far_moves)
    spread = spread_start(amplitude(reduce_end(state), [(width, width)]))
    spread, grad1, back = together((spread, grad1, back))
    last = spread_end(spread_far(spread))
    first, last = together((fold(back), last))
    second = fold(exchange(finish(0, 0, half1, last, grad1), far_moves))
    return jnp.concatenate([first, second], axis=2).transpose(1, 0, 2)


def solution(mesh):
    return jax.shard_map(
        body,
        mesh=mesh,
        in_specs=(P("aux", "orb", None), P("aux", None), P(), P(), P()),
        out_specs=P("aux", "orb", None),
        check_vma=False,
    )
```
